1024 devices in a mesh: dp: 8 (over x, y_lo), wide: 32 (over z), narrow: 4 (over y_hi, core).
Axes of the slice: x: 4, y: 4 (y_hi: 2, y_lo: 2; y = y_hi * 2 + y_lo), z: 32, core: 2. Of those that a mesh axis runs over, the one named last changes fastest.
Arguments:
- grad_parts: bfloat16 [32, 256, 73728], P(('dp', 'narrow'), 'wide'), may hold values from -8 to 8
- weight: bfloat16 [256, 73728], P('wide', ('dp', 'narrow')), may hold values from -12 to 12
- row_state: float32 [256], P('wide'), may hold values from 0.01 to 1
- col_state: float32 [73728], P(('dp', 'narrow')), may hold values from 0.01 to 1
Outputs:
- update: float32 [256, 73728], P('wide', ('dp', 'narrow'))
- new_row_state: float32 [256], P('wide')
- new_col_state: float32 [73728], P(('dp', 'narrow'))
The draws below stay inside these ranges and needn't reach their ends.
All inputs are finite; a program needn't handle non-finite values.
Results may differ from the reference program's by a relative error of at most 0.0003.
Values sent between devices are 32-bit elements; how exact they have to be, the bound alone decides.
A program may use at most 32 MiB of HBM per device.

```python
import math
import jax
import jax.numpy as jnp
from jax import lax

FF = 73728
STEP = 100
ROWS = 256
REPLICAS = 32


def spread_scales(key, count, spread):
    position = jnp.arange(count, dtype=jnp.float32) / count
    rough = jnp.exp(jax.random.uniform(key, (count,), jnp.float32, 0.0, jnp.log(spread)))
    return 3.0 ** position * rough


def draw_grad_parts(key, part):
    key = jax.random.fold_in(key, 11)
    key_rows, key_cols, key_own = jax.random.split(key, 3)
    cols = spread_scales(key_cols, FF, 3.4)
    rows = spread_scales(key_rows, ROWS, 3.4)
    base = jnp.clip(jax.random.normal(key_own, (REPLICAS, ROWS, FF), jnp.float32), -4.0, 4.0)
    factor = 0.1 / jnp.sqrt(jnp.float32(REPLICAS))
    values = jnp.clip(factor * base * rows[None, :, None] * cols[None, None, :], -8.0, 8.0)
    return values.astype(jnp.bfloat16)


def draw_weight(key, part):
    key = jax.random.fold_in(key, 23)
    key_rows, key_cols, key_vals = jax.random.split(key, 3)
    cols = spread_scales(key_cols, FF, 3.4)
    rows = spread_scales(key_rows, ROWS, 3.4)
    base = jnp.clip(jax.random.normal(key_vals, (ROWS, FF), jnp.float32), -4.0, 4.0)
    values = jnp.clip(0.05 * base * rows[:, None] * cols[None, :], -12.0, 12.0)
    return values.astype(jnp.bfloat16)


def block_levels(stream_key, dims, cuts, smallest, high):
    def one(dim, blocks):
        draws = jax.random.uniform(jax.random.fold_in(jax.random.fold_in(stream_key, 6), dim), (blocks,), jnp.float32, smallest / len(cuts), high / len(cuts))
        return jnp.repeat(jnp.exp(draws), dims[dim] // blocks).reshape((-1,) + (1,) * (len(dims) - dim - 1))

    factor_of = one(*cuts[0])
    for cut in cuts[1:]:
        factor_of = factor_of * one(*cut)
    return factor_of


def setup_inputs(seed: int = 0) -> dict:
    arg_keys = jax.random.split(jax.random.key(seed), 5)
    grad_parts = draw_grad_parts(jax.random.fold_in(arg_keys[4], 71), 0)
    weight = draw_weight(jax.random.fold_in(arg_keys[4], 71), 0)
    row_state = jnp.clip(jnp.exp(math.log(1.0) - 4.6051702 * jax.random.uniform(arg_keys[2], (ROWS,), jnp.float32) ** block_levels(arg_keys[2], (ROWS,), ((0, 32),), -0.2, 0.2)), 0.01, 1.0)
    col_state = jnp.clip(jnp.exp(math.log(1.0) - 4.6051702 * jax.random.uniform(arg_keys[3], (FF,), jnp.float32) ** block_levels(arg_keys[3], (FF,), ((0, 32),), -0.2, 0.2)), 0.01, 1.0)
    return {"grad_parts": grad_parts, "weight": weight, "row_state": row_state, "col_state": col_state}


def reference(grad_parts, weight, row_state, col_state):

    def accumulate(total, piece):
        return (total + piece.astype(jnp.float32), None)
    grad, _ = lax.scan(accumulate, jnp.zeros((ROWS, FF), jnp.float32), grad_parts)
    square = grad * grad + 1e-30
    row_mean = lax.optimization_barrier(jnp.mean(square, axis=1))
    col_mean = lax.optimization_barrier(jnp.mean(square, axis=0))
    beta = 1.0 - STEP ** (-0.8)
    new_row_state = beta * row_state + (1.0 - beta) * row_mean
    new_col_state = beta * col_state + (1.0 - beta) * col_mean
    factor = new_row_state[:, None] * new_col_state[None, :]
    scaled = grad / jnp.sqrt(factor)
    clip = jnp.maximum(1.0, jnp.sqrt(jnp.mean(scaled * scaled)))
    weight_f = weight.astype(jnp.float32)
    weight_rms = jnp.maximum(0.001, jnp.sqrt(jnp.mean(weight_f * weight_f)))
    update = weight_rms * scaled / clip
    return (update, new_row_state, new_col_state)
```

```python
import functools

import jax
import jax.numpy as jnp
from jax import lax
from jax.experimental import pallas as pl
from jax.experimental.pallas import tpu as pltpu
from jax.sharding import PartitionSpec as P

FF = 73728
ROWS = 256
STEP = 100
BETA = 1.0 - STEP ** (-0.8)

MESH = pl.DeviceIdType.MESH
F32 = jnp.float32
R = 8
OWN = 2304
HALF = OWN // 2
GROUPS = OWN // 128
PLANE = 32
Z = 32
CUT = 640

ORDER = ((0, 2), (1, 2), (0, 1), (0, 3), (1, 1), (1, 3), (0, 0), (1, 0))


def chip(x, y, z, c):
    return (x * 2 + y % 2, z, (y // 2) * 2 + c)


def kernel(
    g_hbm, w_ref, row_ref, col_ref,
    upd_ref, nrow_ref, ncol_ref,
    gbuf, part, pair, acc, r1, r2, red, s1, s2, grad,
    wsrc, wz, rsrc, rz, zsrc, zr, zg, tsrc, tz,
    load_sem, p_send, p_recv, a_send, a_recv, b_send, b_recv,
    w_send, w_recv, r_send, r_recv, c_send, c_recv, ag_send, ag_recv, t_send, t_recv,
):
    dp = lax.axis_index("dp")
    z = lax.axis_index("wide")
    nr = lax.axis_index("narrow")
    x, y, core = dp // 2, (nr // 2) * 2 + dp % 2, nr % 2
    me = dp * 4 + nr

    load = pltpu.make_async_copy(g_hbm.at[0], gbuf, load_sem)
    load.start()

    def plane_peer(j):
        t = (me + j) % PLANE
        return (t // 4, z, t % 4)

    def z_peer(j):
        return (dp, (z + j) % Z, nr)

    barrier = pltpu.get_barrier_semaphore()

    @pl.loop(1, PLANE)
    def _(j):
        pl.semaphore_signal(barrier, inc=1, device_id=plane_peer(j), device_id_type=MESH)
        pl.semaphore_signal(barrier, inc=1, device_id=z_peer(j), device_id_type=MESH)

    wacc = jnp.zeros((R, 128), F32)
    for k in range(GROUPS):
        wk = w_ref[:, k * 128:(k + 1) * 128].astype(F32)
        wacc = wacc + wk * wk
    wsrc[...] = jnp.sum(wacc, axis=0, keepdims=True)
    load.wait()
    pl.semaphore_wait(barrier, PLANE - 1 + Z - 1)

    def cols(h, d, e, c):
        tx = (x + (d if h == 0 else e)) % 4
        ty = (y + (e if h == 0 else d)) % 4
        owner = ((tx * 2 + ty % 2) * 2 + ty // 2) * 2 + c
        return pl.ds(pl.multiple_of(owner * OWN + h * HALF, 128), HALF)

    other = chip(x, y, z, 1 - core)
    swaps = []
    for i, (h, d) in enumerate(ORDER):
        @pl.loop(0, 4)
        def _(e):
            part[h, d, e] = gbuf[:, cols(h, d, e, 1 - core)].astype(F32)

        copy = pltpu.make_async_remote_copy(
            part.at[h, d], pair.at[h, d], p_send.at[i], p_recv.at[i], other, MESH)
        copy.start()
        swaps.append(copy)

    def near(axis, s):
        if axis == 0:
            return chip((x + 4 + s) % 4, y, z, core)
        return chip(x, (y + 4 + s) % 4, z, core)

    def remote(src, dst, sems, i, device):
        return pltpu.make_async_remote_copy(
            src, dst, sems[0].at[i], sems[1].at[i], device, MESH)

    first = [[None] * 6, [None] * 6]
    for h in range(2):
        sems = (a_send.at[h], a_recv.at[h])
        up, down = near(h, 1), near(h, -1)
        first[h][0] = remote(acc.at[h, 2, pl.ds(0, 2)], r1.at[h, 0], sems, 0, up)
        first[h][1] = remote(acc.at[h, 2, pl.ds(2, 2)], r1.at[h, 1], sems, 1, down)
        first[h][2] = remote(acc.at[h, 1, pl.ds(2, 2)], r2.at[h, 0, pl.ds(2, 2)], sems, 2, up)
        first[h][3] = remote(acc.at[h, 3, pl.ds(0, 2)], r2.at[h, 1, pl.ds(0, 2)], sems, 3, down)
        first[h][4] = remote(acc.at[h, 1, pl.ds(0, 2)], r2.at[h, 0, pl.ds(0, 2)], sems, 4, up)
        first[h][5] = remote(acc.at[h, 3, pl.ds(2, 2)], r2.at[h, 1, pl.ds(2, 2)], sems, 5, down)

    for i, (h, d) in enumerate(ORDER):
        swaps[i].wait_recv()

        @pl.loop(0, 4)
        def _(e):
            acc[h, d, e] = gbuf[:, cols(h, d, e, core)].astype(F32) + pair[h, d, e]

        if d == 2:
            first[h][0].start()
            first[h][1].start()
        elif d == 1:
            first[h][2].start()
        elif d == 3:
            first[h][3].start()

    @pl.loop(1, Z)
    def _(j):
        pltpu.make_async_remote_copy(
            wsrc, wz.at[j - 1], w_send, w_recv, z_peer(j), MESH).start()

    for h in range(2):
        first[h][0].wait_recv()
        for e in range(2):
            acc[h, 1, e] = acc[h, 1, e] + r1[h, 0, e]
        first[h][4].start()
        first[h][1].wait_recv()
        for e in range(2):
            acc[h, 3, 2 + e] = acc[h, 3, 2 + e] + r1[h, 1, e]
        first[h][5].start()

    second = [[None] * 6, [None] * 6]
    lo, hi = pl.ds(0, CUT), pl.ds(CUT, HALF - CUT)
    for h in range(2):
        sems = (b_send.at[h], b_recv.at[h])
        up, down = near(1 - h, 1), near(1 - h, -1)
        second[h][0] = remote(red.at[h, 2, :, lo], s1.at[h, :, lo], sems, 0, up)
        second[h][1] = remote(red.at[h, 2, :, hi], s1.at[h, :, hi], sems, 1, down)
        second[h][2] = remote(red.at[h, 1, :, hi], s2.at[h, 0, :, hi], sems, 2, up)
        second[h][3] = remote(red.at[h, 3, :, lo], s2.at[h, 1, :, lo], sems, 3, down)
        second[h][4] = remote(red.at[h, 1, :, lo], s2.at[h, 0, :, lo], sems, 4, up)
        second[h][5] = remote(red.at[h, 3, :, hi], s2.at[h, 1, :, hi], sems, 5, down)

    for h in range(2):
        for i in range(2, 6):
            first[h][i].wait_recv()
        for e in (2, 1, 3, 0):
            red[h, e] = acc[h, 0, e] + r2[h, 0, e] + r2[h, 1, e]
            if e == 2:
                second[h][0].start()
                second[h][1].start()
            elif e == 1:
                second[h][2].start()
            elif e == 3:
                second[h][3].start()
    for h in range(2):
        second[h][0].wait_recv()
        red[h, 1, :, lo] = red[h, 1, :, lo] + s1[h, :, lo]
        second[h][4].start()
        second[h][1].wait_recv()
        red[h, 3, :, hi] = red[h, 3, :, hi] + s1[h, :, hi]
        second[h][5].start()

    rowacc = jnp.zeros((R, 128), F32)
    for h in range(2):
        for i in range(2, 6):
            second[h][i].wait_recv()
        for k in range(HALF // 128):
            at = pl.ds(k * 128, 128)
            g = red[h, 0, :, at] + s2[h, 0, :, at] + s2[h, 1, :, at]
            grad[:, h * HALF + k * 128:h * HALF + (k + 1) * 128] = g
            rowacc = rowacc + (g * g + 1e-30)

    diagonal = (lax.broadcasted_iota(jnp.int32, (R, 128), 0)
                == lax.broadcasted_iota(jnp.int32, (R, 128), 1))
    rowsum = jnp.sum(rowacc, axis=1, keepdims=True)
    rsrc[...] = jnp.sum(jnp.where(diagonal, rowsum, 0.0), axis=0, keepdims=True)

    @pl.loop(1, PLANE)
    def _(j):
        pltpu.make_async_remote_copy(
            rsrc, rz.at[j - 1], r_send, r_recv, plane_peer(j), MESH).start()

    def all_of(ref, send, recv):
        return pltpu.make_async_remote_copy(ref, ref, send, recv, other, MESH)

    all_of(rz, r_send, r_recv).wait_recv()
    rowtotal = rsrc[...] + jnp.sum(rz[...], axis=0)
    new_row = BETA * row_ref[...] + (1.0 - BETA) * (rowtotal[:, :R] / FF)
    nrow_ref[...] = new_row
    eye = (lax.broadcasted_iota(jnp.int32, (R, R), 0)
           == lax.broadcasted_iota(jnp.int32, (R, R), 1))
    rows = jnp.sum(jnp.where(eye, jnp.broadcast_to(new_row, (R, R)), 0.0), axis=1, keepdims=True)
    inv_rows = jnp.broadcast_to(1.0 / rows, (R, 128))

    for k in range(GROUPS):
        g = grad[:, k * 128:(k + 1) * 128]
        square = g * g
        zsrc[k, 0:1] = jnp.sum(square + 1e-30, axis=0, keepdims=True)
        zsrc[k, 1:2] = jnp.sum(square * inv_rows, axis=0, keepdims=True)

    mine = (9 * z + 15) // 16
    is_owner = ((16 * mine) // 9 == z) & (mine < GROUPS)

    @pl.loop(0, GROUPS)
    def _(k):
        to = (16 * k) // 9

        @pl.when(to != z)
        def _():
            pltpu.make_async_remote_copy(
                zsrc.at[k], zr.at[(z - to + Z) % Z - 1], c_send, c_recv,
                (dp, to, nr), MESH).start()

    @pl.when(is_owner)
    def _():
        all_of(zr, c_send, c_recv).wait_recv()
        own = zsrc[mine] + jnp.sum(zr[...], axis=0)
        col = col_ref[pl.ds(mine, 1), :]
        new_col = BETA * col + (1.0 - BETA) * (own[0:1] / ROWS)
        zg[mine, 0:1] = new_col
        zg[mine, 1:2] = own[1:2] / new_col

        @pl.loop(1, Z)
        def _(j):
            pltpu.make_async_remote_copy(
                zg.at[mine], zg.at[mine], ag_send, ag_recv.at[mine],
                z_peer(j), MESH).start()

    all_of(wz, w_send, w_recv).wait_recv()
    tsrc[1:2] = wsrc[...] + jnp.sum(wz[...], axis=0)
    inv_sqrt_rows = jnp.broadcast_to(lax.rsqrt(rows), (R, 128))

    @pl.loop(0, GROUPS)
    def _(k):
        @pl.when((16 * k) // 9 != z)
        def _():
            pltpu.make_async_remote_copy(
                zg.at[k], zg.at[k], ag_send, ag_recv.at[k], other, MESH).wait_recv()

    tsrc[0:1] = jnp.sum(zg[...], axis=0)[1:2]

    @pl.loop(1, PLANE)
    def _(j):
        pltpu.make_async_remote_copy(
            tsrc, tz.at[j - 1], t_send, t_recv, plane_peer(j), MESH).start()

    for k in range(GROUPS):
        new_col = zg[k, 0:1]
        ncol_ref[k:k + 1] = new_col
        at = slice(k * 128, (k + 1) * 128)
        grad[:, at] = grad[:, at] * inv_sqrt_rows * lax.rsqrt(new_col)

    all_of(tz, t_send, t_recv).wait_recv()
    total = jnp.sum(tsrc[...] + jnp.sum(tz[...], axis=0), axis=1, keepdims=True)
    root = jnp.sqrt(total / (ROWS * FF))
    clip = jnp.maximum(1.0, root[0:1])
    weight_rms = jnp.maximum(0.001, root[1:2])
    upd_ref[...] = grad[...] * (weight_rms / clip)

    for i in range(8):
        swaps[i].wait_send()
    for h in range(2):
        for i in range(6):
            first[h][i].wait_send()
            second[h][i].wait_send()
    all_of(wz, w_send, w_recv).wait_send()
    all_of(rz, r_send, r_recv).wait_send()
    all_of(tz, t_send, t_recv).wait_send()

    @pl.when(is_owner)
    def _():
        all_of(zr.at[pl.ds(0, GROUPS - 1)], c_send, c_recv).wait_send()
        all_of(zr, ag_send, c_recv).wait_send()

    @pl.when(jnp.logical_not(is_owner))
    def _():
        all_of(zr.at[pl.ds(0, GROUPS)], c_send, c_recv).wait_send()


def on_device(grad_parts, weight, row_state, col_state):
    vmem = pl.BlockSpec(memory_space=pltpu.VMEM)
    dma = pltpu.SemaphoreType.DMA
    update, new_row, new_col = pl.pallas_call(
        kernel,
        out_shape=(
            jax.ShapeDtypeStruct((R, OWN), F32),
            jax.ShapeDtypeStruct((1, R), F32),
            jax.ShapeDtypeStruct((GROUPS, 128), F32),
        ),
        in_specs=[pl.BlockSpec(memory_space=pltpu.HBM), vmem, vmem, vmem],
        out_specs=(vmem, vmem, vmem),
        scratch_shapes=[
            pltpu.VMEM((R, FF), jnp.bfloat16),
            pltpu.VMEM((2, 4, 4, R, HALF), F32),
            pltpu.VMEM((2, 4, 4, R, HALF), F32),
            pltpu.VMEM((2, 4, 4, R, HALF), F32),
            pltpu.VMEM((2, 2, 2, R, HALF), F32),
            pltpu.VMEM((2, 2, 4, R, HALF), F32),
            pltpu.VMEM((2, 4, R, HALF), F32),
            pltpu.VMEM((2, R, HALF), F32),
            pltpu.VMEM((2, 2, R, HALF), F32),
            pltpu.VMEM((R, OWN), F32),
            pltpu.VMEM((1, 128), F32),
            pltpu.VMEM((Z - 1, 1, 128), F32),
            pltpu.VMEM((1, 128), F32),
            pltpu.VMEM((PLANE - 1, 1, 128), F32),
            pltpu.VMEM((GROUPS, 2, 128), F32),
            pltpu.VMEM((Z - 1, 2, 128), F32),
            pltpu.VMEM((GROUPS, 2, 128), F32),
            pltpu.VMEM((2, 128), F32),
            pltpu.VMEM((PLANE - 1, 2, 128), F32),
            dma,
            dma((8,)), dma((8,)),
            dma((2, 6)), dma((2, 6)),
            dma((2, 6)), dma((2, 6)),
            dma, dma,
            dma, dma,
            dma, dma,
            dma, dma((GROUPS,)),
            dma, dma,
        ],
        compiler_params=pltpu.CompilerParams(
            collective_id=0, has_side_effects=True, vmem_limit_bytes=48 * 2**20
        ),
    )(grad_parts, weight, row_state.reshape(1, R), col_state.reshape(GROUPS, 128))
    return update, new_row.reshape(R), new_col.reshape(OWN)


def solution(mesh):
    return jax.shard_map(
        on_device,
        mesh=mesh,
        in_specs=(
            P(("dp", "narrow"), "wide", None),
            P("wide", ("dp", "narrow")),
            P("wide"),
            P(("dp", "narrow")),
        ),
        out_specs=(P("wide", ("dp", "narrow")), P("wide"), P(("dp", "narrow"))),
        check_vma=False,
    )
```

```python
import jax
import jax.numpy as jnp
from jax import lax
from jax.experimental import pallas as pl
from jax.experimental.pallas import tpu as pltpu
from jax.sharding import PartitionSpec as P

FF = 73728
ROWS = 256
STEP = 100
BETA = 1.0 - STEP ** (-0.8)

MESH = pl.DeviceIdType.MESH
F32 = jnp.float32
R = 8
OWN = 2304
HALF = OWN // 2
GROUPS = OWN // 128
PLANE = 32
Z = 32
NEAR = 4
CUT = 640

ORDER = ((0, 2), (1, 2), (0, 1), (0, 3), (1, 1), (1, 3), (0, 0), (1, 0))


def chip(x, y, z, c):
    return (x * 2 + y % 2, z, (y // 2) * 2 + c)


def far_first(i, far):
    return far + ((i + 1) // 2) * (2 * ((i + 1) % 2) - 1)


def kernel(
    g_hbm, w_hbm, row_hbm, col_hbm,
    upd_ref, nrow_ref, ncol_ref,
    gbuf, w_ref, row_ref, col_ref, part, pair, acc, r1, r2, red, s1, s2, grad,
    wz, rz, zsrc, zr, zr2, zg, tz,
    load_sem, p_send, p_recv, a_send, a_recv, b_send, b_recv,
    w_send, w_recv, r_send, r_recv, c_send, c_recv, c2_send, c2_recv, ag_send, ag_recv, t_send, t_recv,
    reach4, reach8,
):
    dp = lax.axis_index("dp")
    z = lax.axis_index("wide")
    nr = lax.axis_index("narrow")
    x, y, core = dp // 2, (nr // 2) * 2 + dp % 2, nr % 2
    me = dp * 4 + nr
    other = chip(x, y, z, 1 - core)

    sent = []

    loads = [
        pltpu.make_async_copy(src, dst, load_sem.at[i])
        for i, (src, dst) in enumerate(
            ((g_hbm.at[0], gbuf), (w_hbm, w_ref), (row_hbm, row_ref), (col_hbm, col_ref)))
    ]
    for load in loads:
        load.start()

    def plane_peer(j):
        t = (me + j) % PLANE
        return (t // 4, z, t % 4)

    def z_peer(j):
        return (dp, (z + j) % Z, nr)

    def signal(sem, device):
        pl.semaphore_signal(sem, inc=1, device_id=device, device_id_type=MESH)

    def bytes_of(ref, send, recv):
        return pltpu.make_async_remote_copy(ref, ref, send, recv, other, MESH)

    barrier = pltpu.get_barrier_semaphore()

    @pl.loop(1, PLANE)
    def _(j):
        signal(barrier, plane_peer(j))

    @pl.loop(1, NEAR + 1)
    def _(j):
        signal(barrier, z_peer(j))
        signal(barrier, z_peer(Z - j))

    for load in loads:
        load.wait()

    wacc = jnp.zeros((R, 128), F32)
    for k in range(GROUPS):
        wk = w_ref[:, k * 128:(k + 1) * 128].astype(F32)
        wacc = wacc + wk * wk
    wz[z] = jnp.sum(wacc, axis=0, keepdims=True)

    pl.semaphore_wait(barrier, PLANE - 1 + 2 * NEAR)
    signal(reach4, z_peer(NEAR))
    signal(reach4, z_peer(Z - NEAR))

    def cols(h, d, e, c):
        tx = (x + (d if h == 0 else e)) % 4
        ty = (y + (e if h == 0 else d)) % 4
        owner = ((tx * 2 + ty % 2) * 2 + ty // 2) * 2 + c
        return pl.ds(pl.multiple_of(owner * OWN + h * HALF, 128), HALF)

    swaps = []
    for i, (h, d) in enumerate(ORDER):
        @pl.loop(0, 4)
        def _(e):
            part[h, d, e] = gbuf[:, cols(h, d, e, 1 - core)].astype(F32)

        copy = pltpu.make_async_remote_copy(
            part.at[h, d], pair.at[h, d], p_send.at[i], p_recv.at[i], other, MESH)
        copy.start()
        swaps.append(copy)
        sent.append(copy.wait_send)

    def near(axis, s):
        if axis == 0:
            return chip((x + 4 + s) % 4, y, z, core)
        return chip(x, (y + 4 + s) % 4, z, core)

    def remote(src, dst, sems, i, device):
        return pltpu.make_async_remote_copy(
            src, dst, sems[0].at[i], sems[1].at[i], device, MESH)

    first = [[None] * 6, [None] * 6]
    for h in range(2):
        sems = (a_send.at[h], a_recv.at[h])
        up, down = near(h, 1), near(h, -1)
        first[h][0] = remote(acc.at[h, 2, pl.ds(0, 2)], r1.at[h, 0], sems, 0, up)
        first[h][1] = remote(acc.at[h, 2, pl.ds(2, 2)], r1.at[h, 1], sems, 1, down)
        first[h][2] = remote(acc.at[h, 1, pl.ds(2, 2)], r2.at[h, 0, pl.ds(2, 2)], sems, 2, up)
        first[h][3] = remote(acc.at[h, 3, pl.ds(0, 2)], r2.at[h, 1, pl.ds(0, 2)], sems, 3, down)
        first[h][4] = remote(acc.at[h, 1, pl.ds(0, 2)], r2.at[h, 0, pl.ds(0, 2)], sems, 4, up)
        first[h][5] = remote(acc.at[h, 3, pl.ds(2, 2)], r2.at[h, 1, pl.ds(2, 2)], sems, 5, down)
        sent.extend(copy.wait_send for copy in first[h])

    for i, (h, d) in enumerate(ORDER):
        swaps[i].wait_recv()

        @pl.loop(0, 4)
        def _(e):
            acc[h, d, e] = gbuf[:, cols(h, d, e, core)].astype(F32) + pair[h, d, e]

        if d == 2:
            first[h][0].start()
            first[h][1].start()
        elif d == 1:
            first[h][2].start()
        elif d == 3:
            first[h][3].start()

    pl.semaphore_wait(reach4, 2)
    signal(reach8, z_peer(2 * NEAR))
    signal(reach8, z_peer(Z - 2 * NEAR))

    for h in range(2):
        first[h][0].wait_recv()
        for e in range(2):
            acc[h, 1, e] = acc[h, 1, e] + r1[h, 0, e]
        first[h][4].start()
        first[h][1].wait_recv()
        for e in range(2):
            acc[h, 3, 2 + e] = acc[h, 3, 2 + e] + r1[h, 1, e]
        first[h][5].start()

    second = [[None] * 6, [None] * 6]
    lo, hi = pl.ds(0, CUT), pl.ds(CUT, HALF - CUT)
    for h in range(2):
        sems = (b_send.at[h], b_recv.at[h])
        up, down = near(1 - h, 1), near(1 - h, -1)
        second[h][0] = remote(red.at[h, 2, :, lo], s1.at[h, :, lo], sems, 0, up)
        second[h][1] = remote(red.at[h, 2, :, hi], s1.at[h, :, hi], sems, 1, down)
        second[h][2] = remote(red.at[h, 1, :, hi], s2.at[h, 0, :, hi], sems, 2, up)
        second[h][3] = remote(red.at[h, 3, :, lo], s2.at[h, 1, :, lo], sems, 3, down)
        second[h][4] = remote(red.at[h, 1, :, lo], s2.at[h, 0, :, lo], sems, 4, up)
        second[h][5] = remote(red.at[h, 3, :, hi], s2.at[h, 1, :, hi], sems, 5, down)
        sent.extend(copy.wait_send for copy in second[h])

    for h in range(2):
        for i in range(2, 6):
            first[h][i].wait_recv()
        for e in (2, 1, 3, 0):
            red[h, e] = acc[h, 0, e] + r2[h, 0, e] + r2[h, 1, e]
            if e == 2:
                second[h][0].start()
                second[h][1].start()
            elif e == 1:
                second[h][2].start()
            elif e == 3:
                second[h][3].start()
    for h in range(2):
        second[h][0].wait_recv()
        red[h, 1, :, lo] = red[h, 1, :, lo] + s1[h, :, lo]
        second[h][4].start()
        second[h][1].wait_recv()
        red[h, 3, :, hi] = red[h, 3, :, hi] + s1[h, :, hi]
        second[h][5].start()

    rowacc = jnp.zeros((R, 128), F32)
    for h in range(2):
        for i in range(2, 6):
            second[h][i].wait_recv()
        for k in range(HALF // 128):
            at = pl.ds(k * 128, 128)
            g = red[h, 0, :, at] + s2[h, 0, :, at] + s2[h, 1, :, at]
            grad[:, h * HALF + k * 128:h * HALF + (k + 1) * 128] = g
            rowacc = rowacc + (g * g + 1e-30)

    diagonal = (lax.broadcasted_iota(jnp.int32, (R, 128), 0)
                == lax.broadcasted_iota(jnp.int32, (R, 128), 1))
    rowsum = jnp.sum(rowacc, axis=1, keepdims=True)
    rz[me] = jnp.sum(jnp.where(diagonal, rowsum, 0.0), axis=0, keepdims=True)

    @pl.loop(1, PLANE)
    def _(j):
        pltpu.make_async_remote_copy(
            rz.at[me], rz.at[me], r_send, r_recv, plane_peer(j), MESH).start()

    rest = bytes_of(rz.at[pl.ds(1, PLANE - 1)], r_send, r_recv)
    sent.append(rest.wait_send)
    rest.wait_recv()
    rowtotal = jnp.sum(rz[...], axis=0)
    new_row = BETA * row_ref[...] + (1.0 - BETA) * (rowtotal[:, :R] / FF)
    nrow_ref[...] = new_row
    eye = (lax.broadcasted_iota(jnp.int32, (R, R), 0)
           == lax.broadcasted_iota(jnp.int32, (R, R), 1))
    rows = jnp.sum(jnp.where(eye, jnp.broadcast_to(new_row, (R, R)), 0.0), axis=1, keepdims=True)
    inv_rows = jnp.broadcast_to(1.0 / rows, (R, 128))

    for k in range(GROUPS):
        g = grad[:, k * 128:(k + 1) * 128]
        square = g * g
        zsrc[k, 0:1] = jnp.sum(square + 1e-30, axis=0, keepdims=True)
        zsrc[k, 1:2] = jnp.sum(square * inv_rows, axis=0, keepdims=True)

    pl.semaphore_wait(reach8, 2)

    @pl.loop(0, Z - 1)
    def _(i):
        off = far_first(i, 16)
        pltpu.make_async_remote_copy(
            zsrc.at[(z + off) % 16], zr.at[z], c_send, c_recv, z_peer(off), MESH).start()

    rest_c = bytes_of(zr.at[pl.ds(1, Z - 1)], c_send, c_recv)
    sent.append(rest_c.wait_send)
    twice = z % 8 == 4

    def extra(t):
        return 16 + (t % 16) // 12

    def to_extra(i):
        t = 8 * i + 4
        return t != z, pltpu.make_async_remote_copy(
            zsrc.at[extra(t)], zr2.at[z], c2_send.at[i], c2_recv, (dp, t, nr), MESH)

    @pl.loop(0, 4)
    def _(i):
        needed, copy = to_extra(i)

        @pl.when(needed)
        def _():
            copy.start()

    def sent_extra():
        @pl.loop(0, 4)
        def _(i):
            needed, copy = to_extra(i)

            @pl.when(needed)
            def _():
                copy.wait_send()

    sent.append(sent_extra)

    @pl.loop(0, Z - 1)
    def _(i):
        pltpu.make_async_remote_copy(
            wz.at[z], wz.at[z], w_send, w_recv, z_peer(far_first(i, 16)), MESH).start()

    rest_w = bytes_of(wz.at[pl.ds(1, Z - 1)], w_send, w_recv)
    sent.append(rest_w.wait_send)

    def finish_group(got, k, sem):
        own = jnp.sum(got[...], axis=0)
        new_col = BETA * col_ref[pl.ds(k, 1), :] + (1.0 - BETA) * (own[0:1] / ROWS)
        zg[k, 0:1] = new_col
        zg[k, 1:2] = own[1:2] / new_col

        @pl.loop(0, 15)
        def _(i):
            off = (1 - i % 2) * (Z - 8 + i // 2) + (i % 2) * (7 - i // 2)
            pltpu.make_async_remote_copy(
                zg.at[k], zg.at[k], sem, ag_recv.at[k], z_peer(off), MESH).start()

    def sent_group(sem):
        return bytes_of(zg.at[pl.ds(0, 15)], sem, c_recv).wait_send()

    zr[z] = zsrc[z % 16]
    rest_c.wait_recv()
    finish_group(zr, z % 16, ag_send.at[0])
    sent.append(lambda: sent_group(ag_send.at[0]))

    @pl.when(twice)
    def _():
        zr2[z] = zsrc[extra(z)]
        bytes_of(zr2.at[pl.ds(1, Z - 1)], c_send, c2_recv).wait_recv()
        finish_group(zr2, extra(z), ag_send.at[1])

    def sent_twice():
        @pl.when(twice)
        def _():
            sent_group(ag_send.at[1])

    sent.append(sent_twice)

    inv_sqrt_rows = jnp.broadcast_to(lax.rsqrt(rows), (R, 128))
    for k in range(GROUPS):
        at = slice(k * 128, (k + 1) * 128)
        grad[:, at] = grad[:, at] * inv_sqrt_rows

    @pl.loop(0, GROUPS)
    def _(k):
        local = (k == z % 16) | (twice & (k == extra(z)))

        @pl.when(jnp.logical_not(local))
        def _():
            bytes_of(zg.at[k], c_send, ag_recv.at[k]).wait_recv()

    tz[me, 0:1] = jnp.sum(zg[...], axis=0)[1:2]
    rest_w.wait_recv()
    tz[me, 1:2] = jnp.sum(wz[...], axis=0)

    @pl.loop(1, PLANE)
    def _(j):
        pltpu.make_async_remote_copy(
            tz.at[me], tz.at[me], t_send, t_recv, plane_peer(j), MESH).start()

    rest_t = bytes_of(tz.at[pl.ds(1, PLANE - 1)], t_send, t_recv)
    sent.append(rest_t.wait_send)

    for k in range(GROUPS):
        new_col = zg[k, 0:1]
        ncol_ref[k:k + 1] = new_col
        at = slice(k * 128, (k + 1) * 128)
        grad[:, at] = grad[:, at] * lax.rsqrt(new_col)

    rest_t.wait_recv()
    total = jnp.sum(jnp.sum(tz[...], axis=0), axis=1, keepdims=True)
    root = jnp.sqrt(total / (ROWS * FF))
    clip = jnp.maximum(1.0, root[0:1])
    weight_rms = jnp.maximum(0.001, root[1:2])
    upd_ref[...] = grad[...] * (weight_rms / clip)

    for wait in sent:
        wait()


def on_device(grad_parts, weight, row_state, col_state):
    vmem = pl.BlockSpec(memory_space=pltpu.VMEM)
    dma = pltpu.SemaphoreType.DMA
    args = (grad_parts, weight, row_state.reshape(1, R), col_state.reshape(GROUPS, 128))
    update, new_row, new_col = pl.pallas_call(
        kernel,
        out_shape=(
            jax.ShapeDtypeStruct((R, OWN), F32),
            jax.ShapeDtypeStruct((1, R), F32),
            jax.ShapeDtypeStruct((GROUPS, 128), F32),
        ),
        in_specs=[pl.BlockSpec(memory_space=pltpu.HBM)] * 4,
        out_specs=(vmem, vmem, vmem),
        scratch_shapes=[
            pltpu.VMEM((R, FF), jnp.bfloat16),
            pltpu.VMEM((R, OWN), jnp.bfloat16),
            pltpu.VMEM((1, R), F32),
            pltpu.VMEM((GROUPS, 128), F32),
            pltpu.VMEM((2, 4, 4, R, HALF), F32),
            pltpu.VMEM((2, 4, 4, R, HALF), F32),
            pltpu.VMEM((2, 4, 4, R, HALF), F32),
            pltpu.VMEM((2, 2, 2, R, HALF), F32),
            pltpu.VMEM((2, 2, 4, R, HALF), F32),
            pltpu.VMEM((2, 4, R, HALF), F32),
            pltpu.VMEM((2, R, HALF), F32),
            pltpu.VMEM((2, 2, R, HALF), F32),
            pltpu.VMEM((R, OWN), F32),
            pltpu.VMEM((Z, 1, 128), F32),
            pltpu.VMEM((PLANE, 1, 128), F32),
            pltpu.VMEM((GROUPS, 2, 128), F32),
            pltpu.VMEM((Z, 2, 128), F32),
            pltpu.VMEM((Z, 2, 128), F32),
            pltpu.VMEM((GROUPS, 2, 128), F32),
            pltpu.VMEM((PLANE, 2, 128), F32),
            dma((4,)),
            dma((8,)), dma((8,)),
            dma((2, 6)), dma((2, 6)),
            dma((2, 6)), dma((2, 6)),
            dma, dma,
            dma, dma,
            dma, dma,
            dma((4,)), dma,
            dma((2,)), dma((GROUPS,)),
            dma, dma,
            pltpu.SemaphoreType.REGULAR, pltpu.SemaphoreType.REGULAR,
        ],
        compiler_params=pltpu.CompilerParams(
            collective_id=0, has_side_effects=True, vmem_limit_bytes=48 * 2**20
        ),
    )(*(pltpu.with_memory_space_constraint(a, pltpu.HBM) for a in args))
    return update, new_row.reshape(R), new_col.reshape(OWN)


def solution(mesh):
    return jax.shard_map(
        on_device,
        mesh=mesh,
        in_specs=(
            P(("dp", "narrow"), "wide", None),
            P("wide", ("dp", "narrow")),
            P("wide"),
            P(("dp", "narrow")),
        ),
        out_specs=(P("wide", ("dp", "narrow")), P("wide"), P(("dp", "narrow"))),
        check_vma=False,
    )
```

```python
import jax
import jax.numpy as jnp
from jax import lax
from jax.experimental import pallas as pl
from jax.experimental.pallas import tpu as pltpu
from jax.sharding import PartitionSpec as P

FF = 73728
ROWS = 256
STEP = 100
BETA = 1.0 - STEP ** (-0.8)

MESH = pl.DeviceIdType.MESH
F32 = jnp.float32
R = 8
OWN = 2304
HALF = OWN // 2
GROUPS = OWN // 128
PLANE = 32
Z = 32
COPIES = 2
APART = Z // COPIES
EACH = 16 // APART

ORDER = ((0, 2), (1, 2), (0, 1), (1, 1), (0, 3), (1, 3), (0, 0), (1, 0))


def chip(x, y, z, c):
    return (x * 2 + y % 2, z, (y // 2) * 2 + c)


def far_first(i, far):
    return far + ((i + 1) // 2) * (2 * ((i + 1) % 2) - 1)


def kernel(
    g_hbm, w_hbm, row_hbm, col_hbm,
    upd_ref, nrow_ref, ncol_ref,
    gbuf, w_ref, row_ref, col_ref, part, pair, acc, r1, r2, red, s2, grad,
    wz, rz, csrc, tsrc, cz, tz, cz2, tz2, call, tall, fz,
    load_sem, p_send, p_recv, a_send, a_recv, b_send, b_recv,
    one_send, one_recv, x_send, x_recv, ag_send, ag_recv,
    rows_in, reach2, reach4, reach8,
):
    dp = lax.axis_index("dp")
    z = lax.axis_index("wide")
    nr = lax.axis_index("narrow")
    x, y, core = dp // 2, (nr // 2) * 2 + dp % 2, nr % 2
    me = dp * 4 + nr
    other = chip(x, y, z, 1 - core)

    sent = []

    loads = [
        pltpu.make_async_copy(src, dst, load_sem.at[i])
        for i, (src, dst) in enumerate(
            ((g_hbm.at[0], gbuf), (w_hbm, w_ref), (row_hbm, row_ref), (col_hbm, col_ref)))
    ]
    for load in loads:
        load.start()

    def near(axis, s):
        if axis == 0:
            return chip((x + s) % 4, y, z, core)
        return chip(x, (y + s) % 4, z, core)

    def plane_peer(j):
        t = (me + j) % PLANE
        return (t // 4, z, t % 4)

    def z_peer(j):
        return (dp, (z + j) % Z, nr)

    def signal(sem, device):
        pl.semaphore_signal(sem, inc=1, device_id=device, device_id_type=MESH)

    def remote(src, dst, send, recv, device):
        return pltpu.make_async_remote_copy(src, dst, send, recv, device, MESH)

    def bytes_of(ref, send, recv):
        return remote(ref, ref, send, recv, other)

    barrier = pltpu.get_barrier_semaphore()
    signal(barrier, other)
    for s in (1, 3, 2):
        signal(barrier, near(0, s))
        signal(barrier, near(1, s))
        signal(barrier, chip((x + s) % 4, y, z, 1 - core))
    for s in (1, 2):
        signal(barrier, z_peer(s))
        signal(barrier, z_peer(Z - s))

    for load in loads[1:]:
        load.wait()
    wacc = jnp.zeros((R, 128), F32)
    for k in range(GROUPS):
        wk = w_ref[:, k * 128:(k + 1) * 128].astype(F32)
        wacc = wacc + wk * wk
    wz[z] = jnp.sum(wacc, axis=0, keepdims=True)

    def cols(h, d, e, c):
        tx = (x + (d if h == 0 else e)) % 4
        ty = (y + (e if h == 0 else d)) % 4
        owner = ((tx * 2 + ty % 2) * 2 + ty // 2) * 2 + c
        return pl.ds(pl.multiple_of(owner * OWN + h * HALF, 128), HALF)

    loads[0].wait()
    swaps = []
    for i, (h, d) in enumerate(ORDER):
        for e in range(4):
            part[h, d, e] = gbuf[:, cols(h, d, e, 1 - core)].astype(F32)
        if i == 0:
            pl.semaphore_wait(barrier, 14)
        copy = remote(part.at[h, d], pair.at[h, d], p_send.at[i], p_recv.at[i], other)
        copy.start()
        swaps.append(copy)
        sent.append(copy.wait_send)

    for s in (1, 2, 3):
        signal(rows_in, near(1, s))
    signal(reach2, z_peer(2))
    signal(reach2, z_peer(Z - 2))

    relay = [[None] * 4, [None] * 4]
    straight = [[None] * 4, [None] * 4]
    onward = [[None] * 4, [None] * 4]
    for h in range(2):
        up, down = near(h, 1), near(h, 3)
        for e in range(4):
            with_relay, against = (up, down) if e % 2 == 0 else (down, up)
            to, back = (0, 1) if e % 2 == 0 else (1, 0)
            relay[h][e] = remote(
                acc.at[h, 2, e], r1.at[h, e], a_send.at[h, 0, e], a_recv.at[h, 0, e], with_relay)
            onward[h][e] = remote(
                acc.at[h, 1 + 2 * to, e], r2.at[h, to, e],
                a_send.at[h, 1, e], a_recv.at[h, 1, e], with_relay)
            straight[h][e] = remote(
                acc.at[h, 1 + 2 * back, e], r2.at[h, back, e],
                a_send.at[h, 2, e], a_recv.at[h, 2, e], against)
            sent.extend(c[h][e].wait_send for c in (relay, onward, straight))

    for i, (h, d) in enumerate(ORDER):
        swaps[i].wait_recv()
        for e in (2, 1, 0, 3):
            acc[h, d, e] = gbuf[:, cols(h, d, e, core)].astype(F32) + pair[h, d, e]
            if d == 2:
                relay[h][e].start()
            elif (d, e) in ((1, 1), (1, 3), (3, 2), (3, 0)):
                straight[h][e].start()

    pl.semaphore_wait(reach2, 2)
    signal(reach4, z_peer(4))
    signal(reach4, z_peer(Z - 4))

    for e in (2, 1, 3, 0):
        for h in range(2):
            d = 1 if e % 2 == 0 else 3
            relay[h][e].wait_recv()
            acc[h, d, e] = acc[h, d, e] + r1[h, e]
            onward[h][e].start()

    second = [[None] * 4, [None] * 4]
    for h in range(2):
        for e in range(1, 4):
            second[h][e] = remote(
                red.at[h, e], s2.at[h, e], b_send.at[h, e], b_recv.at[h, e], near(1 - h, e))
            sent.append(second[h][e].wait_send)

    pl.semaphore_wait(reach4, 2)
    signal(reach8, z_peer(8))
    signal(reach8, z_peer(Z - 8))

    for e in (2, 1, 3, 0):
        for h in range(2):
            straight[h][e].wait_recv()
            onward[h][e].wait_recv()
            red[h, e] = acc[h, 0, e] + r2[h, 0, e] + r2[h, 1, e]
            if e:
                second[h][e].start()

    rowacc = jnp.zeros((R, 128), F32)
    for h in range(2):
        for e in (1, 3, 2):
            second[h][e].wait_recv()
        for k in range(HALF // 128):
            at = pl.ds(k * 128, 128)
            g = (red[h, 0, :, at] + s2[h, 1, :, at]) + (s2[h, 3, :, at] + s2[h, 2, :, at])
            grad[:, h * HALF + k * 128:h * HALF + (k + 1) * 128] = g
            rowacc = rowacc + (g * g + 1e-30)

    diagonal = (lax.broadcasted_iota(jnp.int32, (R, 128), 0)
                == lax.broadcasted_iota(jnp.int32, (R, 128), 1))
    rowsum = jnp.sum(rowacc, axis=1, keepdims=True)
    rz[me] = jnp.sum(jnp.where(diagonal, rowsum, 0.0), axis=0, keepdims=True)
    pl.semaphore_wait(rows_in, 3)

    def to_plane(ref, i):
        @pl.loop(0, PLANE - 1)
        def _(j):
            remote(ref.at[me], ref.at[me], one_send.at[i], one_recv.at[i],
                   plane_peer(far_first(j, PLANE // 2))).start()

        rest = bytes_of(ref.at[pl.ds(1, PLANE - 1)], one_send.at[i], one_recv.at[i])
        sent.append(rest.wait_send)
        return rest.wait_recv

    rows_here = to_plane(rz, 0)

    def first_group(t):
        return (t % APART) * EACH

    def owns_extra(t):
        return t % (APART // 2) == APART // 4

    def extra(t):
        return 16 + (t % APART) // (3 * APART // 4)

    def to_owners(src, at_owner, at_extra, i):
        @pl.loop(0, Z - 1)
        def _(j):
            off = far_first(j, Z // 2)
            remote(src.at[pl.ds(first_group(z + off), EACH)], at_owner.at[z],
                   one_send.at[i], one_recv.at[i], z_peer(off)).start()

        rest = bytes_of(at_owner.at[pl.ds(1, Z - 1)], one_send.at[i], one_recv.at[i])
        sent.append(rest.wait_send)

        def copy(j):
            t = j * (APART // 2) + APART // 4
            return t != z, remote(
                src.at[extra(t)], at_extra.at[z], x_send.at[i, j], x_recv.at[i], (dp, t, nr))

        @pl.loop(0, 2 * COPIES)
        def _(j):
            needed, c = copy(j)
            pl.when(needed)(c.start)

        def sent_extra():
            @pl.loop(0, 2 * COPIES)
            def _(j):
                needed, c = copy(j)
                pl.when(needed)(c.wait_send)

        sent.append(sent_extra)
        at_owner[z] = src[pl.ds(first_group(z), EACH)]
        return rest.wait_recv

    def to_near(ref, k, n, send, recv):
        @pl.loop(0, APART - 1)
        def _(j):
            half = APART // 2
            off = (1 - j % 2) * (Z - half + j // 2) + (j % 2) * (half - 1 - j // 2)
            remote(ref.at[pl.ds(k, n)], ref.at[pl.ds(k, n)], send, recv, z_peer(off)).start()

    def from_near(ref, i):
        @pl.loop(0, APART)
        def _(r):
            @pl.when(r != z % APART)
            def _():
                bytes_of(ref.at[pl.ds(0, EACH)], ag_send.at[i, 0], ag_recv.at[i, r]).wait_recv()

        for q in range(2):
            @pl.when(jnp.logical_not(owns_extra(z) & (extra(z) == 16 + q)))
            def _():
                bytes_of(ref.at[0], ag_send.at[i, 0], ag_recv.at[i, APART + q]).wait_recv()

    def sent_near(ref, i):
        def wait():
            bytes_of(ref.at[pl.ds(0, EACH * (APART - 1))], ag_send.at[i, 0], one_recv.at[0]).wait_send()

            @pl.when(owns_extra(z))
            def _():
                bytes_of(ref.at[pl.ds(0, APART - 1)], ag_send.at[i, 1], one_recv.at[0]).wait_send()

        sent.append(wait)

    for k in range(GROUPS):
        g = grad[:, k * 128:(k + 1) * 128]
        csrc[k] = jnp.sum(g * g + 1e-30, axis=0, keepdims=True)
    pl.semaphore_wait(reach8, 2)
    c_here = to_owners(csrc, cz, cz2, 1)

    rows_here()
    rowtotal = jnp.sum(rz[...], axis=0)
    new_row = BETA * row_ref[...] + (1.0 - BETA) * (rowtotal[:, :R] / FF)
    nrow_ref[...] = new_row
    eye = (lax.broadcasted_iota(jnp.int32, (R, R), 0)
           == lax.broadcasted_iota(jnp.int32, (R, R), 1))
    rows = jnp.sum(jnp.where(eye, jnp.broadcast_to(new_row, (R, R)), 0.0), axis=1, keepdims=True)
    inv_rows = jnp.broadcast_to(1.0 / rows, (R, 128))

    for k in range(GROUPS):
        g = grad[:, k * 128:(k + 1) * 128]
        tsrc[k] = jnp.sum(g * g * inv_rows, axis=0, keepdims=True)
    t_here = to_owners(tsrc, tz, tz2, 2)

    @pl.loop(0, Z - 1)
    def _(j):
        remote(wz.at[z], wz.at[z], one_send.at[3], one_recv.at[3],
               z_peer(far_first(j, Z // 2))).start()

    w_here = bytes_of(wz.at[pl.ds(1, Z - 1)], one_send.at[3], one_recv.at[3])
    sent.append(w_here.wait_send)

    inv_sqrt_rows = jnp.broadcast_to(lax.rsqrt(rows), (R, 128))
    for k in range(GROUPS):
        at = slice(k * 128, (k + 1) * 128)
        grad[:, at] = grad[:, at] * inv_sqrt_rows
    for wait in sent:
        wait()
    sent.clear()

    def new_cols(ref, k):
        return BETA * col_ref[pl.ds(k, 1), :] + (1.0 - BETA) * (ref / ROWS)

    c_here()
    own = jnp.sum(cz[...], axis=0)
    for s in range(EACH):
        call[first_group(z) + s] = new_cols(own[s], first_group(z) + s)
    to_near(call, first_group(z), EACH, ag_send.at[0, 0], ag_recv.at[0, z % APART])

    @pl.when(owns_extra(z))
    def _():
        cz2[z] = csrc[extra(z)]
        bytes_of(cz2.at[pl.ds(1, Z - 1)], one_send.at[0], x_recv.at[1]).wait_recv()
        call[extra(z)] = new_cols(jnp.sum(cz2[...], axis=0), extra(z))
        to_near(call, extra(z), 1, ag_send.at[0, 1], ag_recv.at[0, APART + extra(z) - 16])

    sent_near(call, 0)

    t_here()
    own = jnp.sum(tz[...], axis=0)
    for s in range(EACH):
        tall[first_group(z) + s] = own[s] / call[first_group(z) + s]
    to_near(tall, first_group(z), EACH, ag_send.at[1, 0], ag_recv.at[1, z % APART])

    @pl.when(owns_extra(z))
    def _():
        tz2[z] = tsrc[extra(z)]
        bytes_of(tz2.at[pl.ds(1, Z - 1)], one_send.at[0], x_recv.at[2]).wait_recv()
        tall[extra(z)] = jnp.sum(tz2[...], axis=0) / call[extra(z)]
        to_near(tall, extra(z), 1, ag_send.at[1, 1], ag_recv.at[1, APART + extra(z) - 16])

    sent_near(tall, 1)

    from_near(call, 0)
    for k in range(GROUPS):
        new_col = call[k]
        ncol_ref[k:k + 1] = new_col
        at = slice(k * 128, (k + 1) * 128)
        grad[:, at] = grad[:, at] * lax.rsqrt(new_col)
    w_here.wait_recv()
    fz[me, 1:2] = jnp.sum(wz[...], axis=0)

    from_near(tall, 1)
    fz[me, 0:1] = jnp.sum(tall[...], axis=0)
    sums_here = to_plane(fz, 4)
    for wait in sent:
        wait()
    sums_here()
    total = jnp.sum(jnp.sum(fz[...], axis=0), axis=1, keepdims=True)
    root = jnp.sqrt(total / (ROWS * FF))
    clip = jnp.maximum(1.0, root[0:1])
    weight_rms = jnp.maximum(0.001, root[1:2])
    upd_ref[...] = grad[...] * (weight_rms / clip)


def on_device(grad_parts, weight, row_state, col_state):
    vmem = pl.BlockSpec(memory_space=pltpu.VMEM)
    dma = pltpu.SemaphoreType.DMA
    args = (grad_parts, weight, row_state.reshape(1, R), col_state.reshape(GROUPS, 128))
    update, new_row, new_col = pl.pallas_call(
        kernel,
        out_shape=(
            jax.ShapeDtypeStruct((R, OWN), F32),
            jax.ShapeDtypeStruct((1, R), F32),
            jax.ShapeDtypeStruct((GROUPS, 128), F32),
        ),
        in_specs=[pl.BlockSpec(memory_space=pltpu.HBM)] * 4,
        out_specs=(vmem, vmem, vmem),
        scratch_shapes=[
            pltpu.VMEM((R, FF), jnp.bfloat16),
            pltpu.VMEM((R, OWN), jnp.bfloat16),
            pltpu.VMEM((1, R), F32),
            pltpu.VMEM((GROUPS, 128), F32),
            pltpu.VMEM((2, 4, 4, R, HALF), F32),
            pltpu.VMEM((2, 4, 4, R, HALF), F32),
            pltpu.VMEM((2, 4, 4, R, HALF), F32),
            pltpu.VMEM((2, 4, R, HALF), F32),
            pltpu.VMEM((2, 2, 4, R, HALF), F32),
            pltpu.VMEM((2, 4, R, HALF), F32),
            pltpu.VMEM((2, 4, R, HALF), F32),
            pltpu.VMEM((R, OWN), F32),
            pltpu.VMEM((Z, 1, 128), F32),
            pltpu.VMEM((PLANE, 1, 128), F32),
            pltpu.VMEM((GROUPS, 1, 128), F32),
            pltpu.VMEM((GROUPS, 1, 128), F32),
            pltpu.VMEM((Z, EACH, 1, 128), F32),
            pltpu.VMEM((Z, EACH, 1, 128), F32),
            pltpu.VMEM((Z, 1, 128), F32),
            pltpu.VMEM((Z, 1, 128), F32),
            pltpu.VMEM((GROUPS, 1, 128), F32),
            pltpu.VMEM((GROUPS, 1, 128), F32),
            pltpu.VMEM((PLANE, 2, 128), F32),
            dma((4,)),
            dma((8,)), dma((8,)),
            dma((2, 3, 4)), dma((2, 3, 4)),
            dma((2, 4)), dma((2, 4)),
            dma((5,)), dma((5,)),
            dma((3, 2 * COPIES)), dma((3,)),
            dma((2, 2)), dma((2, APART + 2)),
            *[pltpu.SemaphoreType.REGULAR] * 4,
        ],
        compiler_params=pltpu.CompilerParams(
            collective_id=0, has_side_effects=True, vmem_limit_bytes=48 * 2**20
        ),
    )(*(pltpu.with_memory_space_constraint(a, pltpu.HBM) for a in args))
    return update, new_row.reshape(R), new_col.reshape(OWN)


def solution(mesh):
    return jax.shard_map(
        on_device,
        mesh=mesh,
        in_specs=(
            P(("dp", "narrow"), "wide", None),
            P("wide", ("dp", "narrow")),
            P("wide"),
            P(("dp", "narrow")),
        ),
        out_specs=(P("wide", ("dp", "narrow")), P("wide"), P(("dp", "narrow"))),
        check_vma=False,
    )
```

```python
import jax
import jax.numpy as jnp
from jax import lax
from jax.experimental import pallas as pl
from jax.experimental.pallas import tpu as pltpu
from jax.sharding import PartitionSpec as P

FF = 73728
ROWS = 256
STEP = 100
BETA = 1.0 - STEP ** (-0.8)

MESH = pl.DeviceIdType.MESH
F32 = jnp.float32
R = 8
OWN = 2304
HALF = OWN // 2
GROUPS = OWN // 128
PLANE = 32
Z = 32
PAD = 24

ORDER = ((0, 2), (1, 2), (0, 1), (1, 1), (0, 3), (1, 3), (0, 0), (1, 0))


def chip(x, y, z, c):
    return (x * 2 + y % 2, z, (y // 2) * 2 + c)


def far_first(i, far):
    return far + ((i + 1) // 2) * (2 * ((i + 1) % 2) - 1)


def kernel(
    g_hbm, w_hbm, row_hbm, col_hbm,
    upd_ref, nrow_ref, ncol_ref,
    gbuf, w_ref, row_ref, col_ref, part, pair, acc, r1, r2, red, s2, grad,
    rz, csrc, tsrc, cz, tz, call, fz, final,
    load_sem, p_send, p_recv, a_send, a_recv, b_send, b_recv,
    one_send, one_recv, rows_in,
):
    dp = lax.axis_index("dp")
    z = lax.axis_index("wide")
    nr = lax.axis_index("narrow")
    x, y, core = dp // 2, (nr // 2) * 2 + dp % 2, nr % 2
    me = dp * 4 + nr
    other = chip(x, y, z, 1 - core)

    sent = []

    loads = [
        pltpu.make_async_copy(src, dst, load_sem.at[i])
        for i, (src, dst) in enumerate(
            ((g_hbm.at[0], gbuf), (w_hbm, w_ref), (row_hbm, row_ref), (col_hbm, col_ref)))
    ]
    for load in loads:
        load.start()

    def near(axis, s):
        if axis == 0:
            return chip((x + s) % 4, y, z, core)
        return chip(x, (y + s) % 4, z, core)

    def plane_peer(j):
        t = (me + j) % PLANE
        return (t // 4, z, t % 4)

    def signal(sem, device):
        pl.semaphore_signal(sem, inc=1, device_id=device, device_id_type=MESH)

    def remote(src, dst, send, recv, device):
        return pltpu.make_async_remote_copy(src, dst, send, recv, device, MESH)

    def bytes_of(ref, send, recv):
        return remote(ref, ref, send, recv, other)

    barrier = pltpu.get_barrier_semaphore()
    signal(barrier, other)
    for s in (1, 3, 2):
        signal(barrier, near(0, s))
        signal(barrier, near(1, s))
        signal(barrier, chip((x + s) % 4, y, z, 1 - core))

    @pl.when(z == 0)
    def _():
        @pl.loop(1, Z)
        def _(j):
            signal(barrier, (dp, j, nr))

    for load in loads[1:]:
        load.wait()
    wacc = jnp.zeros((R, 128), F32)
    for k in range(GROUPS):
        wk = w_ref[:, k * 128:(k + 1) * 128].astype(F32)
        wacc = wacc + wk * wk
    wsum = jnp.sum(wacc, axis=0, keepdims=True)

    def cols(h, d, e, c):
        tx = (x + (d if h == 0 else e)) % 4
        ty = (y + (e if h == 0 else d)) % 4
        owner = ((tx * 2 + ty % 2) * 2 + ty // 2) * 2 + c
        return pl.ds(pl.multiple_of(owner * OWN + h * HALF, 128), HALF)

    loads[0].wait()
    swaps = []
    for i, (h, d) in enumerate(ORDER):
        for e in range(4):
            part[h, d, e] = gbuf[:, cols(h, d, e, 1 - core)].astype(F32)
        if i == 0:
            pl.when(z == 0)(lambda: pl.semaphore_wait(barrier, 10))
            pl.when(z != 0)(lambda: pl.semaphore_wait(barrier, 11))
        copy = remote(part.at[h, d], pair.at[h, d], p_send.at[i], p_recv.at[i], other)
        copy.start()
        swaps.append(copy)
        sent.append(copy.wait_send)

    for s in (1, 2, 3):
        signal(rows_in, near(1, s))

    relay = [[None] * 4, [None] * 4]
    straight = [[None] * 4, [None] * 4]
    onward = [[None] * 4, [None] * 4]
    for h in range(2):
        up, down = near(h, 1), near(h, 3)
        for e in range(4):
            with_relay, against = (up, down) if e % 2 == 0 else (down, up)
            to, back = (0, 1) if e % 2 == 0 else (1, 0)
            relay[h][e] = remote(
                acc.at[h, 2, e], r1.at[h, e], a_send.at[h, 0, e], a_recv.at[h, 0, e], with_relay)
            onward[h][e] = remote(
                acc.at[h, 1 + 2 * to, e], r2.at[h, to, e],
                a_send.at[h, 1, e], a_recv.at[h, 1, e], with_relay)
            straight[h][e] = remote(
                acc.at[h, 1 + 2 * back, e], r2.at[h, back, e],
                a_send.at[h, 2, e], a_recv.at[h, 2, e], against)
            sent.extend(c[h][e].wait_send for c in (relay, onward, straight))

    for i, (h, d) in enumerate(ORDER):
        swaps[i].wait_recv()
        for e in (2, 1, 0, 3):
            acc[h, d, e] = gbuf[:, cols(h, d, e, core)].astype(F32) + pair[h, d, e]
            if d == 2:
                relay[h][e].start()
            elif (d, e) in ((1, 1), (1, 3), (3, 2), (3, 0)):
                straight[h][e].start()

    for e in (2, 1, 3, 0):
        for h in range(2):
            d = 1 if e % 2 == 0 else 3
            relay[h][e].wait_recv()
            acc[h, d, e] = acc[h, d, e] + r1[h, e]
            onward[h][e].start()

    second = [[None] * 4, [None] * 4]
    for h in range(2):
        for e in range(1, 4):
            second[h][e] = remote(
                red.at[h, e], s2.at[h, e], b_send.at[h, e], b_recv.at[h, e], near(1 - h, e))
            sent.append(second[h][e].wait_send)

    for e in (2, 1, 3, 0):
        for h in range(2):
            straight[h][e].wait_recv()
            onward[h][e].wait_recv()
            red[h, e] = acc[h, 0, e] + r2[h, 0, e] + r2[h, 1, e]
            if e:
                second[h][e].start()

    rowacc = jnp.zeros((R, 128), F32)
    for h in range(2):
        for e in (1, 3, 2):
            second[h][e].wait_recv()
        for k in range(HALF // 128):
            at = pl.ds(k * 128, 128)
            g = (red[h, 0, :, at] + s2[h, 1, :, at]) + (s2[h, 3, :, at] + s2[h, 2, :, at])
            grad[:, h * HALF + k * 128:h * HALF + (k + 1) * 128] = g
            rowacc = rowacc + (g * g + 1e-30)

    diagonal = (lax.broadcasted_iota(jnp.int32, (R, 128), 0)
                == lax.broadcasted_iota(jnp.int32, (R, 128), 1))
    rowsum = jnp.sum(rowacc, axis=1, keepdims=True)
    tsrc[GROUPS:] = jnp.zeros((PAD - GROUPS, 128), F32)
    rz[me] = jnp.sum(jnp.where(diagonal, rowsum, 0.0), axis=0, keepdims=True)
    pl.semaphore_wait(rows_in, 3)

    def to_plane(ref, i):
        @pl.loop(0, PLANE - 1)
        def _(j):
            remote(ref.at[me], ref.at[me], one_send.at[i], one_recv.at[i],
                   plane_peer(far_first(j, PLANE // 2))).start()

        rest = bytes_of(ref.at[pl.ds(1, PLANE - 1)], one_send.at[i], one_recv.at[i])
        sent.append(rest.wait_send)
        return rest.wait_recv

    rows_here = to_plane(rz, 0)

    base = z == 0
    to_base = (dp, 0, nr)

    def send_all(src, dst, i):
        @pl.loop(1, Z)
        def _(j):
            t = (j % 2) * ((j + 1) // 2) + (1 - j % 2) * (Z - j // 2)
            remote(src, dst, one_send.at[i], one_recv.at[i], (dp, t, nr)).start()

    csrc[GROUPS:] = jnp.broadcast_to(wsum, (PAD - GROUPS, 128))
    for k in range(GROUPS):
        g = grad[:, k * 128:(k + 1) * 128]
        csrc[k:k + 1] = jnp.sum(g * g + 1e-30, axis=0, keepdims=True)
    c_copy = remote(csrc, cz.at[z], one_send.at[1], one_recv.at[1], to_base)
    t_copy = remote(tsrc, tz.at[z], one_send.at[2], one_recv.at[2], to_base)

    @pl.when(jnp.logical_not(base))
    def _():
        c_copy.start()

    rows_here()
    rowtotal = jnp.sum(rz[...], axis=0)
    new_row = BETA * row_ref[...] + (1.0 - BETA) * (rowtotal[:, :R] / FF)
    eye = (lax.broadcasted_iota(jnp.int32, (R, R), 0)
           == lax.broadcasted_iota(jnp.int32, (R, R), 1))
    rows = jnp.sum(jnp.where(eye, jnp.broadcast_to(new_row, (R, R)), 0.0), axis=1, keepdims=True)
    inv_rows = jnp.broadcast_to(1.0 / rows, (R, 128))

    for k in range(GROUPS):
        g = grad[:, k * 128:(k + 1) * 128]
        tsrc[k:k + 1] = jnp.sum(g * g * inv_rows, axis=0, keepdims=True)

    @pl.when(jnp.logical_not(base))
    def _():
        t_copy.start()

    nrow_ref[...] = new_row
    inv_sqrt_rows = jnp.broadcast_to(lax.rsqrt(rows), (R, 128))
    for k in range(GROUPS):
        at = slice(k * 128, (k + 1) * 128)
        grad[:, at] = grad[:, at] * inv_sqrt_rows
    for wait in sent:
        wait()
    sent.clear()

    @pl.when(base)
    def _():
        cz[0] = csrc[...]
        bytes_of(cz.at[pl.ds(1, Z - 1)], one_send.at[1], one_recv.at[1]).wait_recv()
        sums = jnp.sum(cz[...], axis=0)
        col = BETA * col_ref[...] + (1.0 - BETA) * (sums[:GROUPS] / ROWS)
        call[0:GROUPS] = col
        call[GROUPS:] = jnp.zeros((PAD - GROUPS, 128), F32)
        send_all(call, call, 5)
        fz[me, 1:2] = sums[GROUPS:GROUPS + 1]
        tz[0] = tsrc[...]
        bytes_of(tz.at[pl.ds(1, Z - 1)], one_send.at[1], one_recv.at[2]).wait_recv()
        total = jnp.sum(tz[...], axis=0)[:GROUPS] / col
        fz[me, 0:1] = jnp.sum(total, axis=0, keepdims=True)
        sums_here = to_plane(fz, 4)
        del sent[:]
        sums_here()
        final[...] = jnp.sum(fz[...], axis=0)
        send_all(final, final, 6)

    @pl.when(jnp.logical_not(base))
    def _():
        c_copy.wait_send()
        t_copy.wait_send()
        bytes_of(call, one_send.at[1], one_recv.at[5]).wait_recv()

    for k in range(GROUPS):
        new_col = call[k:k + 1]
        at = slice(k * 128, (k + 1) * 128)
        grad[:, at] = grad[:, at] * lax.rsqrt(new_col)
    ncol_ref[...] = call[0:GROUPS]

    @pl.when(jnp.logical_not(base))
    def _():
        bytes_of(final, one_send.at[1], one_recv.at[6]).wait_recv()

    root = jnp.sqrt(jnp.sum(final[...], axis=1, keepdims=True) / (ROWS * FF))
    clip = jnp.maximum(1.0, root[0:1])
    weight_rms = jnp.maximum(0.001, root[1:2])
    upd_ref[...] = grad[...] * (weight_rms / clip)

    @pl.when(base)
    def _():
        bytes_of(cz.at[pl.ds(1, Z - 1)], one_send.at[5], one_recv.at[5]).wait_send()
        bytes_of(fz.at[pl.ds(1, PLANE - 1)], one_send.at[4], one_recv.at[4]).wait_send()
        bytes_of(fz.at[pl.ds(1, Z - 1)], one_send.at[6], one_recv.at[6]).wait_send()


def on_device(grad_parts, weight, row_state, col_state):
    vmem = pl.BlockSpec(memory_space=pltpu.VMEM)
    dma = pltpu.SemaphoreType.DMA
    args = (grad_parts, weight, row_state.reshape(1, R), col_state.reshape(GROUPS, 128))
    update, new_row, new_col = pl.pallas_call(
        kernel,
        out_shape=(
            jax.ShapeDtypeStruct((R, OWN), F32),
            jax.ShapeDtypeStruct((1, R), F32),
            jax.ShapeDtypeStruct((GROUPS, 128), F32),
        ),
        in_specs=[pl.BlockSpec(memory_space=pltpu.HBM)] * 4,
        out_specs=(vmem, vmem, vmem),
        scratch_shapes=[
            pltpu.VMEM((R, FF), jnp.bfloat16),
            pltpu.VMEM((R, OWN), jnp.bfloat16),
            pltpu.VMEM((1, R), F32),
            pltpu.VMEM((GROUPS, 128), F32),
            pltpu.VMEM((2, 4, 4, R, HALF), F32),
            pltpu.VMEM((2, 4, 4, R, HALF), F32),
            pltpu.VMEM((2, 4, 4, R, HALF), F32),
            pltpu.VMEM((2, 4, R, HALF), F32),
            pltpu.VMEM((2, 2, 4, R, HALF), F32),
            pltpu.VMEM((2, 4, R, HALF), F32),
            pltpu.VMEM((2, 4, R, HALF), F32),
            pltpu.VMEM((R, OWN), F32),
            pltpu.VMEM((PLANE, 1, 128), F32),
            pltpu.VMEM((PAD, 128), F32),
            pltpu.VMEM((PAD, 128), F32),
            pltpu.VMEM((Z, PAD, 128), F32),
            pltpu.VMEM((Z, PAD, 128), F32),
            pltpu.VMEM((PAD, 128), F32),
            pltpu.VMEM((PLANE, 2, 128), F32),
            pltpu.VMEM((2, 128), F32),
            dma((4,)),
            dma((8,)), dma((8,)),
            dma((2, 3, 4)), dma((2, 3, 4)),
            dma((2, 4)), dma((2, 4)),
            dma((7,)), dma((7,)),
            pltpu.SemaphoreType.REGULAR,
        ],
        compiler_params=pltpu.CompilerParams(
            collective_id=0, has_side_effects=True, vmem_limit_bytes=48 * 2**20
        ),
    )(*(pltpu.with_memory_space_constraint(a, pltpu.HBM) for a in args))
    return update, new_row.reshape(R), new_col.reshape(OWN)


def solution(mesh):
    return jax.shard_map(
        on_device,
        mesh=mesh,
        in_specs=(
            P(("dp", "narrow"), "wide", None),
            P("wide", ("dp", "narrow")),
            P("wide"),
            P(("dp", "narrow")),
        ),
        out_specs=(P("wide", ("dp", "narrow")), P("wide"), P(("dp", "narrow"))),
        check_vma=False,
    )
```

```python
import jax
import jax.numpy as jnp
from jax import lax
from jax.experimental import pallas as pl
from jax.experimental.pallas import tpu as pltpu
from jax.sharding import PartitionSpec as P

FF = 73728
ROWS = 256
STEP = 100
BETA = 1.0 - STEP ** (-0.8)

MESH = pl.DeviceIdType.MESH
F32 = jnp.float32
R = 8
OWN = 2304
HALF = OWN // 2
GROUPS = OWN // 128
PLANE = 32
Z = 32
SOON = 4
PAD = 24

ORDER = ((0, 2), (1, 2), (0, 1), (1, 1), (0, 3), (1, 3), (0, 0), (1, 0))


def chip(x, y, z, c):
    return (x * 2 + y % 2, z, (y // 2) * 2 + c)


def far_first(i, far):
    return far + ((i + 1) // 2) * (2 * ((i + 1) % 2) - 1)


def kernel(
    g_hbm, w_hbm, row_hbm, col_hbm,
    upd_ref, nrow_ref, ncol_ref,
    gbuf, w_ref, row_ref, col_ref, part, pair, acc, r1, r2, red, s2, grad,
    rz, csrc, tsrc, cz, tz, call, fz, final,
    load_sem, p_send, p_recv, a_send, a_recv, b_send, b_recv,
    one_send, one_recv, plane_in,
):
    dp = lax.axis_index("dp")
    z = lax.axis_index("wide")
    nr = lax.axis_index("narrow")
    x, y, core = dp // 2, (nr // 2) * 2 + dp % 2, nr % 2
    me = dp * 4 + nr
    other = chip(x, y, z, 1 - core)

    sent = []

    def slab(i):
        at = pl.ds(pl.multiple_of(((x + (2, 1, 3, 0)[i]) % 4) * (FF // 4), 128), FF // 4)
        return g_hbm.at[0, :, at], gbuf.at[:, at]

    loads = [
        pltpu.make_async_copy(src, dst, load_sem.at[i])
        for i, (src, dst) in enumerate(
            (slab(0), slab(1), slab(2), slab(3),
             (w_hbm, w_ref), (row_hbm, row_ref), (col_hbm, col_ref)))
    ]
    for load in loads:
        load.start()

    def near(axis, s):
        if axis == 0:
            return chip((x + s) % 4, y, z, core)
        return chip(x, (y + s) % 4, z, core)

    def plane_peer(j):
        t = (me + j) % PLANE
        return (t // 4, z, t % 4)

    def signal(sem, device):
        pl.semaphore_signal(sem, inc=1, device_id=device, device_id_type=MESH)

    def remote(src, dst, send, recv, device):
        return pltpu.make_async_remote_copy(src, dst, send, recv, device, MESH)

    def bytes_of(ref, send, recv):
        return remote(ref, ref, send, recv, other)

    beside = (other, near(0, 1), near(0, 3), near(1, 1), near(1, 3))
    barrier = pltpu.get_barrier_semaphore()
    for device in beside:
        signal(barrier, device)

    @pl.when(z == 0)
    def _():
        @pl.loop(1, Z)
        def _(j):
            signal(barrier, (dp, j, nr))

    def cols(h, d, e, c):
        tx = (x + (d if h == 0 else e)) % 4
        ty = (y + (e if h == 0 else d)) % 4
        owner = ((tx * 2 + ty % 2) * 2 + ty // 2) * 2 + c
        return pl.ds(pl.multiple_of(owner * OWN + h * HALF, 128), HALF)

    swaps = []
    for i, (h, d) in enumerate(ORDER):
        for load in loads[:1] if i == 0 else loads[1:4] if i == 1 else ():
            load.wait()
        for e in range(4):
            part[h, d, e] = gbuf[:, cols(h, d, e, 1 - core)].astype(F32)
        if i == 0:
            pl.when(z == 0)(lambda: pl.semaphore_wait(barrier, 5))
            pl.when(z != 0)(lambda: pl.semaphore_wait(barrier, 6))
        copy = remote(part.at[h, d], pair.at[h, d], p_send.at[i], p_recv.at[i], other)
        copy.start()
        swaps.append(copy)
        sent.append(copy.wait_send)

    def tell(r):
        if r > 0:
            pl.semaphore_wait(plane_in.at[r - 1], 5)
        if r < 4:
            for device in beside:
                signal(plane_in.at[r], device)

    tell(0)

    relay = [[None] * 4, [None] * 4]
    straight = [[None] * 4, [None] * 4]
    onward = [[None] * 4, [None] * 4]
    for h in range(2):
        up, down = near(h, 1), near(h, 3)
        for e in range(4):
            with_relay, against = (up, down) if e % 2 == 0 else (down, up)
            to, back = (0, 1) if e % 2 == 0 else (1, 0)
            relay[h][e] = remote(
                acc.at[h, 2, e], r1.at[h, e], a_send.at[h, 0, e], a_recv.at[h, 0, e], with_relay)
            onward[h][e] = remote(
                acc.at[h, 1 + 2 * to, e], r2.at[h, to, e],
                a_send.at[h, 1, e], a_recv.at[h, 1, e], with_relay)
            straight[h][e] = remote(
                acc.at[h, 1 + 2 * back, e], r2.at[h, back, e],
                a_send.at[h, 2, e], a_recv.at[h, 2, e], against)
            sent.extend(c[h][e].wait_send for c in (relay, onward, straight))

    for i, (h, d) in enumerate(ORDER):
        swaps[i].wait_recv()
        for e in (2, 1, 0, 3):
            acc[h, d, e] = gbuf[:, cols(h, d, e, core)].astype(F32) + pair[h, d, e]
            if d == 2:
                relay[h][e].start()

    for e in (1, 2, 3, 0):
        for h in range(2):
            straight[h][e].start()

    tell(1)

    for load in loads[4:]:
        load.wait()
    wacc = jnp.zeros((R, 128), F32)
    for k in range(GROUPS):
        wk = w_ref[:, k * 128:(k + 1) * 128].astype(F32)
        wacc = wacc + wk * wk
    wsum = jnp.sum(wacc, axis=0, keepdims=True)

    for e in (2, 1, 3, 0):
        for h in range(2):
            d = 1 if e % 2 == 0 else 3
            relay[h][e].wait_recv()
            acc[h, d, e] = acc[h, d, e] + r1[h, e]
            onward[h][e].start()

    tell(2)

    second = [[None] * 4, [None] * 4]
    for h in range(2):
        for e in range(1, 4):
            second[h][e] = remote(
                red.at[h, e], s2.at[h, e], b_send.at[h, e], b_recv.at[h, e], near(1 - h, e))
            sent.append(second[h][e].wait_send)

    for e in (2, 1, 3, 0):
        for h in range(2):
            straight[h][e].wait_recv()
            onward[h][e].wait_recv()
            red[h, e] = acc[h, 0, e] + r2[h, 0, e] + r2[h, 1, e]
            if e:
                second[h][e].start()

    tell(3)
    rowacc = jnp.zeros((R, 128), F32)
    for h in range(2):
        for e in (1, 3, 2):
            second[h][e].wait_recv()
        for k in range(HALF // 128):
            at = pl.ds(k * 128, 128)
            g = (red[h, 0, :, at] + s2[h, 1, :, at]) + (s2[h, 3, :, at] + s2[h, 2, :, at])
            grad[:, h * HALF + k * 128:h * HALF + (k + 1) * 128] = g
            rowacc = rowacc + (g * g + 1e-30)

    diagonal = (lax.broadcasted_iota(jnp.int32, (R, 128), 0)
                == lax.broadcasted_iota(jnp.int32, (R, 128), 1))
    rowsum = jnp.sum(rowacc, axis=1, keepdims=True)
    tsrc[GROUPS:] = jnp.zeros((PAD - GROUPS, 128), F32)
    rz[me] = jnp.sum(jnp.where(diagonal, rowsum, 0.0), axis=0, keepdims=True)
    tell(4)

    def to_plane(ref, i):
        @pl.loop(0, PLANE - 1)
        def _(j):
            remote(ref.at[me], ref.at[me], one_send.at[i], one_recv.at[i],
                   plane_peer(far_first(j, PLANE // 2))).start()

        rest = bytes_of(ref.at[pl.ds(1, PLANE - 1)], one_send.at[i], one_recv.at[i])
        sent.append(rest.wait_send)
        return rest.wait_recv

    rows_here = to_plane(rz, 0)

    base = z == 0
    to_base = (dp, 0, nr)

    def send_along(ref, i, first, last):
        @pl.loop(first, last)
        def _(j):
            remote(ref, ref, one_send.at[i], one_recv.at[i], (dp, j, nr)).start()

    csrc[GROUPS:] = jnp.broadcast_to(wsum, (PAD - GROUPS, 128))
    for k in range(GROUPS):
        g = grad[:, k * 128:(k + 1) * 128]
        csrc[k:k + 1] = jnp.sum(g * g + 1e-30, axis=0, keepdims=True)
    c_copy = remote(csrc, cz.at[z], one_send.at[1], one_recv.at[1], to_base)
    t_copy = remote(tsrc, tz.at[z], one_send.at[2], one_recv.at[2], to_base)

    @pl.when(jnp.logical_not(base))
    def _():
        c_copy.start()

    rows_here()
    rowtotal = jnp.sum(rz[...], axis=0)
    new_row = BETA * row_ref[...] + (1.0 - BETA) * (rowtotal[:, :R] / FF)
    eye = (lax.broadcasted_iota(jnp.int32, (R, R), 0)
           == lax.broadcasted_iota(jnp.int32, (R, R), 1))
    rows = jnp.sum(jnp.where(eye, jnp.broadcast_to(new_row, (R, R)), 0.0), axis=1, keepdims=True)
    inv_rows = jnp.broadcast_to(1.0 / rows, (R, 128))

    for k in range(GROUPS):
        g = grad[:, k * 128:(k + 1) * 128]
        tsrc[k:k + 1] = jnp.sum(g * g * inv_rows, axis=0, keepdims=True)

    @pl.when(jnp.logical_not(base))
    def _():
        t_copy.start()

    nrow_ref[...] = new_row
    inv_sqrt_rows = jnp.broadcast_to(lax.rsqrt(rows), (R, 128))
    for k in range(GROUPS):
        at = slice(k * 128, (k + 1) * 128)
        grad[:, at] = grad[:, at] * inv_sqrt_rows
    for wait in sent:
        wait()
    sent.clear()

    @pl.when(base)
    def _():
        cz[0] = csrc[...]
        bytes_of(cz.at[pl.ds(1, Z - 1)], one_send.at[1], one_recv.at[1]).wait_recv()
        sums = jnp.sum(cz[...], axis=0)
        col = BETA * col_ref[...] + (1.0 - BETA) * (sums[:GROUPS] / ROWS)
        call[0:GROUPS] = col
        call[GROUPS:] = jnp.zeros((PAD - GROUPS, 128), F32)
        send_along(call, 5, 1, Z)
        inv_col = 1.0 / col
        fz[me, 1:2] = sums[GROUPS:GROUPS + 1]
        tz[0] = tsrc[...]
        bytes_of(tz.at[pl.ds(1, Z - 1)], one_send.at[1], one_recv.at[2]).wait_recv()
        total = jnp.sum(tz[...], axis=0)[:GROUPS] * inv_col
        fz[me, 0:1] = jnp.sum(total, axis=0, keepdims=True)
        sums_here = to_plane(fz, 4)
        sent.clear()

        @pl.loop(0, PLANE)
        def _(j):
            for t in range(1, SOON):
                remote(fz.at[me], fz.at[me], one_send.at[7], one_recv.at[4],
                       (j // 4, t, j % 4)).start()

        bytes_of(cz.at[pl.ds(1, Z - 1)], one_send.at[5], one_recv.at[5]).wait_send()
        bytes_of(fz.at[pl.ds(1, PLANE - 1)], one_send.at[4], one_recv.at[4]).wait_send()
        bytes_of(tz.at[pl.ds(0, 2 * PLANE * (SOON - 1) // PAD)], one_send.at[7], one_recv.at[4]).wait_send()
        sums_here()
        final[...] = jnp.sum(fz[...], axis=0)

    @pl.when(jnp.logical_not(base))
    def _():
        c_copy.wait_send()
        t_copy.wait_send()
        bytes_of(call, one_send.at[1], one_recv.at[5]).wait_recv()

    for k in range(GROUPS):
        new_col = call[k:k + 1]
        at = slice(k * 128, (k + 1) * 128)
        grad[:, at] = grad[:, at] * lax.rsqrt(new_col)
    ncol_ref[...] = call[0:GROUPS]

    @pl.when(z >= SOON)
    def _():
        bytes_of(final, one_send.at[1], one_recv.at[6]).wait_recv()

    @pl.when((z > 0) & (z < SOON))
    def _():
        bytes_of(fz, one_send.at[1], one_recv.at[4]).wait_recv()
        final[...] = jnp.sum(fz[...], axis=0)

    @pl.when(z == SOON - 1)
    def _():
        send_along(final, 6, SOON, Z)

    root = jnp.sqrt(jnp.sum(final[...], axis=1, keepdims=True) / (ROWS * FF))
    clip = jnp.maximum(1.0, root[0:1])
    weight_rms = jnp.maximum(0.001, root[1:2])
    upd_ref[...] = grad[...] * (weight_rms / clip)

    @pl.when(z == SOON - 1)
    def _():
        bytes_of(fz.at[pl.ds(0, Z - SOON)], one_send.at[6], one_recv.at[6]).wait_send()


def on_device(grad_parts, weight, row_state, col_state):
    vmem = pl.BlockSpec(memory_space=pltpu.VMEM)
    dma = pltpu.SemaphoreType.DMA
    args = (grad_parts, weight, row_state.reshape(1, R), col_state.reshape(GROUPS, 128))
    update, new_row, new_col = pl.pallas_call(
        kernel,
        out_shape=(
            jax.ShapeDtypeStruct((R, OWN), F32),
            jax.ShapeDtypeStruct((1, R), F32),
            jax.ShapeDtypeStruct((GROUPS, 128), F32),
        ),
        in_specs=[pl.BlockSpec(memory_space=pltpu.HBM)] * 4,
        out_specs=(vmem, vmem, vmem),
        scratch_shapes=[
            pltpu.VMEM((R, FF), jnp.bfloat16),
            pltpu.VMEM((R, OWN), jnp.bfloat16),
            pltpu.VMEM((1, R), F32),
            pltpu.VMEM((GROUPS, 128), F32),
            pltpu.VMEM((2, 4, 4, R, HALF), F32),
            pltpu.VMEM((2, 4, 4, R, HALF), F32),
            pltpu.VMEM((2, 4, 4, R, HALF), F32),
            pltpu.VMEM((2, 4, R, HALF), F32),
            pltpu.VMEM((2, 2, 4, R, HALF), F32),
            pltpu.VMEM((2, 4, R, HALF), F32),
            pltpu.VMEM((2, 4, R, HALF), F32),
            pltpu.VMEM((R, OWN), F32),
            pltpu.VMEM((PLANE, 1, 128), F32),
            pltpu.VMEM((PAD, 128), F32),
            pltpu.VMEM((PAD, 128), F32),
            pltpu.VMEM((Z, PAD, 128), F32),
            pltpu.VMEM((Z, PAD, 128), F32),
            pltpu.VMEM((PAD, 128), F32),
            pltpu.VMEM((PLANE, 2, 128), F32),
            pltpu.VMEM((2, 128), F32),
            dma((7,)),
            dma((8,)), dma((8,)),
            dma((2, 3, 4)), dma((2, 3, 4)),
            dma((2, 4)), dma((2, 4)),
            dma((8,)), dma((8,)),
            pltpu.SemaphoreType.REGULAR((4,)),
        ],
        compiler_params=pltpu.CompilerParams(
            collective_id=0, has_side_effects=True, vmem_limit_bytes=48 * 2**20
        ),
    )(*(pltpu.with_memory_space_constraint(a, pltpu.HBM) for a in args))
    return update, new_row.reshape(R), new_col.reshape(OWN)


def solution(mesh):
    return jax.shard_map(
        on_device,
        mesh=mesh,
        in_specs=(
            P(("dp", "narrow"), "wide", None),
            P("wide", ("dp", "narrow")),
            P("wide"),
            P(("dp", "narrow")),
        ),
        out_specs=(P("wide", ("dp", "narrow")), P("wide"), P(("dp", "narrow"))),
        check_vma=False,
    )
```

```python
import jax
import jax.numpy as jnp
from jax import lax
from jax.experimental import pallas as pl
from jax.experimental.pallas import tpu as pltpu
from jax.sharding import PartitionSpec as P

FF = 73728
ROWS = 256
STEP = 100
BETA = 1.0 - STEP ** (-0.8)

MESH = pl.DeviceIdType.MESH
F32 = jnp.float32
R = 8
OWN = 2304
HALF = OWN // 2
GROUPS = OWN // 128
PLANE = 32
Z = 32
SOON = 4
PAD = 24

ORDER = ((0, 2), (1, 2), (0, 1), (1, 1), (0, 3), (1, 3), (0, 0), (1, 0))


def chip(x, y, z, c):
    return (x * 2 + y % 2, z, (y // 2) * 2 + c)


def far_first(i, far):
    return far + ((i + 1) // 2) * (2 * ((i + 1) % 2) - 1)


def kernel(
    g_hbm, w_hbm, row_hbm, col_hbm,
    upd_ref, nrow_ref, ncol_ref,
    gbuf, w_ref, row_ref, col_ref, part, pair, acc, r1, r2, red, s2, grad,
    rz, csrc, tsrc, cz, tz, call, fz, final,
    load_sem, p_send, p_recv, a_send, a_recv, b_send, b_recv,
    one_send, one_recv, plane_in,
):
    dp = lax.axis_index("dp")
    z = lax.axis_index("wide")
    nr = lax.axis_index("narrow")
    x, y, core = dp // 2, (nr // 2) * 2 + dp % 2, nr % 2
    me = dp * 4 + nr
    other = chip(x, y, z, 1 - core)

    sent = []

    def slab(i):
        at = pl.ds(pl.multiple_of(((x + (2, 1, 3, 0)[i]) % 4) * (FF // 4), 128), FF // 4)
        return g_hbm.at[0, :, at], gbuf.at[:, at]

    loads = [
        pltpu.make_async_copy(src, dst, load_sem.at[i])
        for i, (src, dst) in enumerate(
            (slab(0), slab(1), slab(2), slab(3),
             (w_hbm, w_ref), (row_hbm, row_ref), (col_hbm, col_ref)))
    ]

    def near(axis, s):
        if axis == 0:
            return chip((x + s) % 4, y, z, core)
        return chip(x, (y + s) % 4, z, core)

    def plane_peer(j):
        t = (me + j) % PLANE
        return (t // 4, z, t % 4)

    def signal(sem, device):
        pl.semaphore_signal(sem, inc=1, device_id=device, device_id_type=MESH)

    def remote(src, dst, send, recv, device):
        return pltpu.make_async_remote_copy(src, dst, send, recv, device, MESH)

    def bytes_of(ref, send, recv):
        return remote(ref, ref, send, recv, other)

    beside = (other, near(0, 1), near(0, 3), near(1, 1), near(1, 3))
    barrier = pltpu.get_barrier_semaphore()
    for device in beside:
        signal(barrier, device)

    for load in loads:
        load.start()

    @pl.when(z == 0)
    def _():
        @pl.loop(1, Z)
        def _(j):
            signal(barrier, (dp, j, nr))

    def cols(h, d, e, c):
        tx = (x + (d if h == 0 else e)) % 4
        ty = (y + (e if h == 0 else d)) % 4
        owner = ((tx * 2 + ty % 2) * 2 + ty // 2) * 2 + c
        return pl.ds(pl.multiple_of(owner * OWN + h * HALF, 128), HALF)

    swaps = []
    for i, (h, d) in enumerate(ORDER):
        for load in loads[:1] if i == 0 else loads[1:4] if i == 1 else ():
            load.wait()
        for e in range(4):
            part[h, d, e] = gbuf[:, cols(h, d, e, 1 - core)].astype(F32)
        if i == 0:
            pl.when(z == 0)(lambda: pl.semaphore_wait(barrier, 5))
            pl.when(z != 0)(lambda: pl.semaphore_wait(barrier, 6))
        copy = remote(part.at[h, d], pair.at[h, d], p_send.at[i], p_recv.at[i], other)
        copy.start()
        swaps.append(copy)
        sent.append(copy.wait_send)

    def tell(r):
        if r > 0:
            pl.semaphore_wait(plane_in.at[r - 1], 5)
        if r < 4:
            for device in beside:
                signal(plane_in.at[r], device)

    tell(0)

    relay = [[None] * 4, [None] * 4]
    straight = [[None] * 4, [None] * 4]
    onward = [[None] * 4, [None] * 4]
    for h in range(2):
        up, down = near(h, 1), near(h, 3)
        for e in range(4):
            with_relay, against = (up, down) if e % 2 == 0 else (down, up)
            to, back = (0, 1) if e % 2 == 0 else (1, 0)
            relay[h][e] = remote(
                acc.at[h, 2, e], r1.at[h, e], a_send.at[h, 0, e], a_recv.at[h, 0, e], with_relay)
            onward[h][e] = remote(
                acc.at[h, 1 + 2 * to, e], r2.at[h, to, e],
                a_send.at[h, 1, e], a_recv.at[h, 1, e], with_relay)
            straight[h][e] = remote(
                acc.at[h, 1 + 2 * back, e], r2.at[h, back, e],
                a_send.at[h, 2, e], a_recv.at[h, 2, e], against)
            sent.extend(c[h][e].wait_send for c in (relay, onward, straight))

    for i, (h, d) in enumerate(ORDER):
        swaps[i].wait_recv()
        for e in (2, 1, 0, 3):
            acc[h, d, e] = gbuf[:, cols(h, d, e, core)].astype(F32) + pair[h, d, e]
            if d == 2:
                relay[h][e].start()

    for e in (1, 2, 3, 0):
        for h in range(2):
            straight[h][e].start()

    tell(1)

    for load in loads[4:]:
        load.wait()
    wacc = jnp.zeros((R, 128), F32)
    for k in range(GROUPS):
        wk = w_ref[:, k * 128:(k + 1) * 128].astype(F32)
        wacc = wacc + wk * wk
    wsum = jnp.sum(wacc, axis=0, keepdims=True)

    for e in (2, 1, 3, 0):
        for h in range(2):
            d = 1 if e % 2 == 0 else 3
            relay[h][e].wait_recv()
            acc[h, d, e] = acc[h, d, e] + r1[h, e]
            onward[h][e].start()

    tell(2)

    second = [[None] * 4, [None] * 4]
    for h in range(2):
        for e in range(1, 4):
            second[h][e] = remote(
                red.at[h, e], s2.at[h, e], b_send.at[h, e], b_recv.at[h, e], near(1 - h, e))
            sent.append(second[h][e].wait_send)

    for e in (2, 1, 3, 0):
        for h in range(2):
            straight[h][e].wait_recv()
            onward[h][e].wait_recv()
            red[h, e] = acc[h, 0, e] + r2[h, 0, e] + r2[h, 1, e]
            if e:
                second[h][e].start()

    tell(3)
    rowacc = jnp.zeros((R, 128), F32)
    for h in range(2):
        for e in (1, 3, 2):
            second[h][e].wait_recv()
        for k in range(HALF // 128):
            at = pl.ds(k * 128, 128)
            g = (red[h, 0, :, at] + s2[h, 1, :, at]) + (s2[h, 3, :, at] + s2[h, 2, :, at])
            grad[:, h * HALF + k * 128:h * HALF + (k + 1) * 128] = g
            rowacc = rowacc + (g * g + 1e-30)

    diagonal = (lax.broadcasted_iota(jnp.int32, (R, 128), 0)
                == lax.broadcasted_iota(jnp.int32, (R, 128), 1))
    rowsum = jnp.sum(rowacc, axis=1, keepdims=True)
    tsrc[GROUPS:] = jnp.zeros((PAD - GROUPS, 128), F32)
    rz[me] = jnp.sum(jnp.where(diagonal, rowsum, 0.0), axis=0, keepdims=True)
    tell(4)

    def to_plane(ref, i):
        @pl.loop(0, PLANE - 1)
        def _(j):
            remote(ref.at[me], ref.at[me], one_send.at[i], one_recv.at[i],
                   plane_peer(far_first(j, PLANE // 2))).start()

        rest = bytes_of(ref.at[pl.ds(1, PLANE - 1)], one_send.at[i], one_recv.at[i])
        sent.append(rest.wait_send)
        return rest.wait_recv

    rows_here = to_plane(rz, 0)

    base = z == 0
    to_base = (dp, 0, nr)

    def send_along(ref, i, first, last):
        @pl.loop(first, last)
        def _(j):
            remote(ref, ref, one_send.at[i], one_recv.at[i], (dp, j, nr)).start()

    csrc[GROUPS:] = jnp.broadcast_to(wsum, (PAD - GROUPS, 128))
    for k in range(GROUPS):
        g = grad[:, k * 128:(k + 1) * 128]
        csrc[k:k + 1] = jnp.sum(g * g + 1e-30, axis=0, keepdims=True)
    c_copy = remote(csrc, cz.at[z], one_send.at[1], one_recv.at[1], to_base)
    t_copy = remote(tsrc, tz.at[z], one_send.at[2], one_recv.at[2], to_base)

    @pl.when(jnp.logical_not(base))
    def _():
        c_copy.start()

    rows_here()
    rowtotal = jnp.sum(rz[...], axis=0)
    new_row = BETA * row_ref[...] + (1.0 - BETA) * (rowtotal[:, :R] / FF)
    eye = (lax.broadcasted_iota(jnp.int32, (R, R), 0)
           == lax.broadcasted_iota(jnp.int32, (R, R), 1))
    rows = jnp.sum(jnp.where(eye, jnp.broadcast_to(new_row, (R, R)), 0.0), axis=1, keepdims=True)
    inv_rows = jnp.broadcast_to(1.0 / rows, (R, 128))

    for first_group in range(0, PAD, 8):
        for k in range(first_group, min(first_group + 8, GROUPS)):
            g = grad[:, k * 128:(k + 1) * 128]
            tsrc[k:k + 1] = jnp.sum(g * g * inv_rows, axis=0, keepdims=True)
        tile = pl.ds(first_group, 8)
        piece = remote(tsrc.at[tile], tz.at[z, tile], one_send.at[2], one_recv.at[2], to_base)
        pl.when(jnp.logical_not(base))(piece.start)

    nrow_ref[...] = new_row
    inv_sqrt_rows = jnp.broadcast_to(lax.rsqrt(rows), (R, 128))
    for k in range(GROUPS):
        at = slice(k * 128, (k + 1) * 128)
        grad[:, at] = grad[:, at] * inv_sqrt_rows
    for wait in sent:
        wait()
    sent.clear()

    @pl.when(base)
    def _():
        cz[0] = csrc[...]
        bytes_of(cz.at[pl.ds(1, Z - 1)], one_send.at[1], one_recv.at[1]).wait_recv()
        sums = jnp.sum(cz[...], axis=0)
        col = BETA * col_ref[...] + (1.0 - BETA) * (sums[:GROUPS] / ROWS)
        call[0:GROUPS] = col
        call[GROUPS:] = jnp.zeros((PAD - GROUPS, 128), F32)
        send_along(call, 5, 1, Z)
        inv_col = 1.0 / col
        fz[me, 1:2] = sums[GROUPS:GROUPS + 1]
        tz[0] = tsrc[...]
        bytes_of(tz.at[pl.ds(1, Z - 1)], one_send.at[1], one_recv.at[2]).wait_recv()
        total = jnp.sum(tz[...], axis=0)[:GROUPS] * inv_col
        fz[me, 0:1] = jnp.sum(total, axis=0, keepdims=True)
        sums_here = to_plane(fz, 4)
        sent.clear()

        @pl.loop(0, PLANE)
        def _(j):
            for t in range(1, SOON):
                remote(fz.at[me], fz.at[me], one_send.at[7], one_recv.at[4],
                       (j // 4, t, j % 4)).start()

        bytes_of(cz.at[pl.ds(1, Z - 1)], one_send.at[5], one_recv.at[5]).wait_send()
        bytes_of(fz.at[pl.ds(1, PLANE - 1)], one_send.at[4], one_recv.at[4]).wait_send()
        bytes_of(tz.at[pl.ds(0, 2 * PLANE * (SOON - 1) // PAD)], one_send.at[7], one_recv.at[4]).wait_send()
        sums_here()
        final[...] = jnp.sum(fz[...], axis=0)

    @pl.when(jnp.logical_not(base))
    def _():
        c_copy.wait_send()
        t_copy.wait_send()
        bytes_of(call, one_send.at[1], one_recv.at[5]).wait_recv()

    for k in range(GROUPS):
        new_col = call[k:k + 1]
        at = slice(k * 128, (k + 1) * 128)
        grad[:, at] = grad[:, at] * lax.rsqrt(new_col)
    ncol_ref[...] = call[0:GROUPS]

    @pl.when(z >= SOON)
    def _():
        bytes_of(final, one_send.at[1], one_recv.at[6]).wait_recv()

    @pl.when((z > 0) & (z < SOON))
    def _():
        bytes_of(fz, one_send.at[1], one_recv.at[4]).wait_recv()
        final[...] = jnp.sum(fz[...], axis=0)

    @pl.when(z == SOON - 1)
    def _():
        send_along(final, 6, SOON, Z)

    root = jnp.sqrt(jnp.sum(final[...], axis=1, keepdims=True) / (ROWS * FF))
    clip = jnp.maximum(1.0, root[0:1])
    weight_rms = jnp.maximum(0.001, root[1:2])
    upd_ref[...] = grad[...] * (weight_rms / clip)

    @pl.when(z == SOON - 1)
    def _():
        bytes_of(fz.at[pl.ds(0, Z - SOON)], one_send.at[6], one_recv.at[6]).wait_send()


def on_device(grad_parts, weight, row_state, col_state):
    vmem = pl.BlockSpec(memory_space=pltpu.VMEM)
    dma = pltpu.SemaphoreType.DMA
    args = (grad_parts, weight, row_state.reshape(1, R), col_state.reshape(GROUPS, 128))
    update, new_row, new_col = pl.pallas_call(
        kernel,
        out_shape=(
            jax.ShapeDtypeStruct((R, OWN), F32),
            jax.ShapeDtypeStruct((1, R), F32),
            jax.ShapeDtypeStruct((GROUPS, 128), F32),
        ),
        in_specs=[pl.BlockSpec(memory_space=pltpu.HBM)] * 4,
        out_specs=(vmem, vmem, vmem),
        scratch_shapes=[
            pltpu.VMEM((R, FF), jnp.bfloat16),
            pltpu.VMEM((R, OWN), jnp.bfloat16),
            pltpu.VMEM((1, R), F32),
            pltpu.VMEM((GROUPS, 128), F32),
            pltpu.VMEM((2, 4, 4, R, HALF), F32),
            pltpu.VMEM((2, 4, 4, R, HALF), F32),
            pltpu.VMEM((2, 4, 4, R, HALF), F32),
            pltpu.VMEM((2, 4, R, HALF), F32),
            pltpu.VMEM((2, 2, 4, R, HALF), F32),
            pltpu.VMEM((2, 4, R, HALF), F32),
            pltpu.VMEM((2, 4, R, HALF), F32),
            pltpu.VMEM((R, OWN), F32),
            pltpu.VMEM((PLANE, 1, 128), F32),
            pltpu.VMEM((PAD, 128), F32),
            pltpu.VMEM((PAD, 128), F32),
            pltpu.VMEM((Z, PAD, 128), F32),
            pltpu.VMEM((Z, PAD, 128), F32),
            pltpu.VMEM((PAD, 128), F32),
            pltpu.VMEM((PLANE, 2, 128), F32),
            pltpu.VMEM((2, 128), F32),
            dma((7,)),
            dma((8,)), dma((8,)),
            dma((2, 3, 4)), dma((2, 3, 4)),
            dma((2, 4)), dma((2, 4)),
            dma((8,)), dma((8,)),
            pltpu.SemaphoreType.REGULAR((4,)),
        ],
        compiler_params=pltpu.CompilerParams(
            collective_id=0, has_side_effects=True, vmem_limit_bytes=48 * 2**20
        ),
    )(*(pltpu.with_memory_space_constraint(a, pltpu.HBM) for a in args))
    return update, new_row.reshape(R), new_col.reshape(OWN)


def solution(mesh):
    return jax.shard_map(
        on_device,
        mesh=mesh,
        in_specs=(
            P(("dp", "narrow"), "wide", None),
            P("wide", ("dp", "narrow")),
            P("wide"),
            P(("dp", "narrow")),
        ),
        out_specs=(P("wide", ("dp", "narrow")), P("wide"), P(("dp", "narrow"))),
        check_vma=False,
    )
```
